32 devices in a mesh: band: 4 (over y, x), dev: 8 (over z, core).
Axes of the slice: x: 2, y: 2, z: 4, core: 2. Of those that a mesh axis runs over, the one named last changes fastest.
Arguments:
- drive: float32 [2, 32, 16384], P(None, None, ('band', 'dev')), may hold values from -6 to 6
- coords: float32 [3, 16384], P(None, ('band', 'dev')), may hold values from 0 to 3
- rule_index: int32 [16384], P(('band', 'dev')), may hold values from 0 to 3
- rule_weight: float32 [4], replicated, may hold values from 0.1 to 0.4
- pair_cols: int32 [3072], P(('band', 'dev')), may hold values from 0 to 63, as said below
- pair_count: int32 [32], P(('band', 'dev')), may hold values from 12 to 96, as said below
Outputs:
- near_field: float32 [2, 32, 16384], P(None, None, ('band', 'dev'))
The draws below stay inside these ranges and needn't reach their ends.
Inputs may be any that keep to these rules, and one draw needn't show every extreme that they name: `pair_cols`: for slot s of device k the listed block column lies from k * 2 + (s mod 2) up to that row plus 16 - 1; slots s < 2 list the diagonal pair. `pair_count`: some device has all 96 slots live.
All inputs are finite; a program needn't handle non-finite values.
Results may differ from the reference program's by a relative error of at most 0.0003.
Values sent between devices are 32-bit elements; how exact they have to be, the bound alone decides.
No kernel may reach another device: no remote copies, remote signals or barrier semaphores. Data moves between devices by JAX's collectives and lax.ppermute only.
A program may use at most 64 MiB of HBM per device.

```python
import math
import jax
import jax.numpy as jnp
from jax import lax

BLOCK = 256
NRHS = 32
RULES = 4
BR_DEV = 2
TILE_DEV = 96
NB = 64
BAND_ROWS = 16
UNKNOWNS = 16384


def draw_pair_cols(key, part):
    slot_ids = jnp.arange(NB // BR_DEV * TILE_DEV, dtype=jnp.int32)
    local_slot = slot_ids % TILE_DEV
    row_block = slot_ids // TILE_DEV * BR_DEV + local_slot % BR_DEV
    offsets = jax.random.randint(key, slot_ids.shape, 0, BAND_ROWS, dtype=jnp.int32)
    offsets = jnp.where(local_slot < BR_DEV, 0, offsets)
    return row_block + offsets % (NB - row_block)


def draw_pair_count(key, part):
    devices = NB // BR_DEV
    first_draw = jax.random.randint(jax.random.fold_in(key, 1), (devices,), TILE_DEV // 8, TILE_DEV + 1, dtype=jnp.int32)
    second_draw = jax.random.randint(jax.random.fold_in(key, 2), (devices,), TILE_DEV // 8, TILE_DEV + 1, dtype=jnp.int32)
    counts = jnp.minimum(first_draw, second_draw)
    chosen = jax.random.randint(jax.random.fold_in(key, 3), (), 0, devices, dtype=jnp.int32)
    device_ids = jnp.arange(devices, dtype=jnp.int32)
    counts = jnp.where(device_ids == chosen, TILE_DEV, counts)
    counts = jnp.where(device_ids == (chosen + 1) % devices, TILE_DEV // 8, counts)
    return counts


def with_ends(entries, key, low, largest):
    place = [jax.random.randint(jax.random.fold_in(key, axis), (), 0, length) for axis, length in enumerate(entries.shape)]
    main_axis = entries.shape.index(max(entries.shape))
    beside = place[:main_axis] + [(place[main_axis] + 1) % entries.shape[main_axis]] + place[main_axis + 1:]
    return entries.at[tuple(place)].set(low).at[tuple(beside)].set(largest)


def levels(key, shape, shards, low, top_value):
    factor_of, own = 1.0, jax.random.fold_in(key, 6)
    for axis_at, blocks in shards:
        heights = jnp.exp(jax.random.uniform(jax.random.fold_in(own, axis_at), (blocks,), jnp.float32, low / len(shards), top_value / len(shards)))
        factor_of = factor_of * jnp.repeat(heights, shape[axis_at] // blocks).reshape([-1 if axis == axis_at else 1 for axis in range(len(shape))])
    return factor_of


def noise(rng, dims, width, most, pieces=(), held_as=jnp.bfloat16):
    result = jax.random.normal(rng, dims, jnp.float32) * width
    if len(pieces) > 0:
        result = levels(rng, dims, pieces, -0.22, 0.18) * result
    return jnp.clip(result, min=-most, max=most).astype(held_as)


def setup_inputs(seed: int = 0) -> dict:
    arg_keys = jax.random.split(jax.random.key(seed), 7)
    drive = noise(arg_keys[0], (2, NRHS, UNKNOWNS), 1.0, 6.0, ((2, 32),), jnp.float32)
    coords = jnp.clip(3.0 * jax.random.uniform(arg_keys[1], (3, UNKNOWNS), jnp.float32) ** levels(arg_keys[1], (3, UNKNOWNS), ((1, 32),), -0.2, 0.2), 0.0, 3.0)
    rule_index = with_ends(jax.random.randint(arg_keys[2], (UNKNOWNS,), 0, RULES), jax.random.fold_in(arg_keys[2], 1), 0, RULES - 1).astype(jnp.int32)
    rule_weight = jnp.clip(jnp.exp(jax.random.uniform(arg_keys[3], (RULES,), jnp.float32, math.log(0.1), math.log(0.4))), 0.1, 0.4)
    pair_cols = draw_pair_cols(jax.random.fold_in(arg_keys[6], 71), 0)
    pair_count = draw_pair_count(jax.random.fold_in(arg_keys[6], 71), 0)
    return {"drive": drive, "coords": coords, "rule_index": rule_index, "rule_weight": rule_weight, "pair_cols": pair_cols, "pair_count": pair_count}


wave_number = 25.0
smoothing = 0.05
highest = lax.Precision.HIGHEST

def point_weights(rule_index, rule_weight):
    matches = rule_index[:, None] == jnp.arange(RULES, dtype=jnp.int32)[None, :]
    return lax.optimization_barrier(jnp.sum(jnp.where(matches, rule_weight[None, :], jnp.zeros_like(rule_weight)[None, :]), axis=1))

def assemble(near_points, far_points, near_w, far_w):
    offsets = near_points[:, :, None] - far_points[:, None, :]
    distance = jnp.sqrt(lax.optimization_barrier(jnp.sum(offsets * offsets, axis=0)) + smoothing * smoothing)
    strength = near_w[:, None] * far_w[None, :] / (4.0 * math.pi * distance)
    phases = wave_number * distance
    return (strength * jnp.cos(phases), strength * jnp.sin(phases))

def complex_apply(vectors, real_part, imag_part, patterns):
    stacked = vectors.reshape(2 * patterns, vectors.shape[2])
    real_prod = jnp.dot(stacked, real_part, precision=highest, preferred_element_type=jnp.float32)
    imag_prod = jnp.dot(stacked, imag_part, precision=highest, preferred_element_type=jnp.float32)
    return jnp.stack([real_prod[:patterns] - imag_prod[patterns:], real_prod[patterns:] + imag_prod[:patterns]])

def add_block(near_field, update_block, block_index):
    previous = lax.dynamic_slice_in_dim(near_field, block_index * BLOCK, BLOCK, 2)
    return lax.dynamic_update_slice_in_dim(near_field, previous + update_block, block_index * BLOCK, 2)

def reference(drive, coords, rule_index, rule_weight, pair_cols, pair_count):
    weights = point_weights(rule_index, rule_weight)
    patterns = drive.shape[1]
    slot_ids = jnp.arange(NB // BR_DEV * TILE_DEV, dtype=jnp.int32)
    owner_dev = slot_ids // TILE_DEV
    local_slot = slot_ids % TILE_DEV
    row_blocks = (owner_dev * BR_DEV + local_slot % BR_DEV).astype(jnp.int32)
    is_live = local_slot < pair_count[owner_dev]

    def one_tile(near_field, entry_item):
        row_block, col_block, alive = entry_item
        near_x = lax.dynamic_slice_in_dim(drive, row_block * BLOCK, BLOCK, 2)
        far_x = lax.dynamic_slice_in_dim(drive, col_block * BLOCK, BLOCK, 2)
        near_points = lax.dynamic_slice_in_dim(coords, row_block * BLOCK, BLOCK, 1)
        far_points = lax.dynamic_slice_in_dim(coords, col_block * BLOCK, BLOCK, 1)
        near_w = lax.dynamic_slice_in_dim(weights, row_block * BLOCK, BLOCK, 0)
        far_w = lax.dynamic_slice_in_dim(weights, col_block * BLOCK, BLOCK, 0)
        real_part, imag_part = assemble(near_points, far_points, near_w, far_w)
        keep_mask = jnp.where(alive, 1.0, 0.0).astype(drive.dtype)
        mirror = jnp.where(alive & (row_block != col_block), 1.0, 0.0).astype(drive.dtype)
        direct = complex_apply(far_x, real_part.T, imag_part.T, patterns) * keep_mask
        mirrored = complex_apply(near_x, real_part, imag_part, patterns) * mirror
        near_field = add_block(near_field, direct, row_block)
        near_field = add_block(near_field, mirrored, col_block)
        return (near_field, None)
    near_field, _ = lax.scan(one_tile, jnp.zeros_like(drive), (row_blocks, pair_cols.astype(jnp.int32), is_live))
    return near_field
```

```python
import functools
import math

import jax
import jax.numpy as jnp
from jax import lax
from jax.experimental import pallas as pl
from jax.experimental.pallas import tpu as pltpu
from jax.sharding import PartitionSpec as P

BLOCK = 256
STRIP = 16
VMEM_LIMIT = 48 * 1024 * 1024

wave_number = 25.0
smoothing = 0.05
per_unit = wave_number / (2.0 * math.pi)
core_sq = (smoothing * per_unit) ** 2
amplitude = per_unit / (4.0 * math.pi)
SINE = (4.4428679, -7.30744342, 3.59478806, -0.78437397)
COSINE = (1.4142135, -6.97885099, 5.73946117, -1.88356297, 0.31069815)

COUNT_ROW = 3
WEIGHT_ROW = 4
EXTRA = 8


def horner(z, terms):
    value = z * terms[-1] + terms[-2]
    for term in terms[-3::-1]:
        value = value * z + term
    return value


def wave(near, far):
    square = None
    for a, b in zip(near, far):
        gap = a - b
        gap = gap * gap
        square = gap + core_sq if square is None else square + gap
    inverse = lax.rsqrt(square)
    turns = square * inverse
    part = turns - jnp.round(turns)
    z = part * part
    s = horner(z, SINE) * part
    scaled = inverse * s
    return inverse - scaled * s, scaled * horner(z, COSINE)


def pack_kernel(width, drive, coords, rules, rule_weight, pair_cols, pair_count, out):
    patterns = drive.shape[1]
    first_row = (lax.axis_index("band") * lax.axis_size("dev") + lax.axis_index("dev")) * 2
    weight = jnp.zeros(rules.shape, jnp.float32)
    for rule in range(rule_weight.shape[0]):
        weight = jnp.where(rules[...] == rule, rule_weight[rule], weight)
    scale = weight * amplitude
    out[0:patterns, :] = drive[0] * scale
    out[patterns : 2 * patterns, :] = drive[1] * scale
    lanes = lax.broadcasted_iota(jnp.int32, rules.shape, 1)

    def count(slot, totals):
        odd = lax.rem(slot, 2)
        place = pair_cols[slot] - first_row - odd + odd * width
        return totals + jnp.where(lanes == place, 1.0, 0.0)

    counts = lax.fori_loop(0, pair_count[0], count, jnp.zeros(rules.shape, jnp.float32))
    base = 2 * patterns
    out[base : base + EXTRA, :] = jnp.zeros((EXTRA, out.shape[1]), jnp.float32)
    out[base : base + 3, :] = coords[...] * per_unit
    out[base + COUNT_ROW : base + COUNT_ROW + 1, :] = counts
    out[base + WEIGHT_ROW : base + WEIGHT_ROW + 1, :] = weight


def near_kernel(groups, first_block, blocks, width, has_start, *refs):
    cols = refs[:blocks]
    points = refs[blocks : blocks + 3]
    refs = refs[blocks + 3 :]
    start, refs = (refs[0], refs[1:]) if has_start else (None, refs)
    out, left, across, row_points, hi_a, lo_a, hi_b, lo_b, acc, tables, plan, factor, sem = refs
    base = cols[0].shape[0] - EXTRA
    half = base // 2
    lanes = tables.shape[2]
    n_rows = 2 * len(groups)
    copies = [
        pltpu.make_async_copy(
            cols[s].at[base : base + EXTRA, 0:lanes], tables.at[s], sem.at[s]
        )
        for s in range(blocks)
    ] + [
        pltpu.make_async_copy(
            points[g].at[:, 0:lanes], tables.at[blocks + g], sem.at[blocks + g]
        )
        for g in range(2)
    ]
    for copy in copies:
        copy.start()
    for s in range(blocks):
        for h in range(2):
            span = slice(h * BLOCK, (h + 1) * BLOCK)
            x = cols[s][0:base, span]
            wide = jnp.concatenate([x, jnp.concatenate([-x[half:], x[:half]], 0)], 1)
            hi = wide.astype(jnp.bfloat16)
            left[2 * s + h, 0:base, :] = hi
            left[2 * s + h, base : 2 * base, :] = (wide - hi.astype(jnp.float32)).astype(
                jnp.bfloat16
            )
            across[2 * s + h, :, 0:EXTRA] = cols[s][base : base + EXTRA, span].T
    for k, g in enumerate(groups):
        for r in range(2):
            row_points[2 * k + r] = points[g + 1][:, r * BLOCK : (r + 1) * BLOCK]
            if has_start:
                acc[2 * k + r] = start[k, :, r * BLOCK : (r + 1) * BLOCK]
            else:
                acc[2 * k + r] = jnp.zeros(acc.shape[1:], jnp.float32)
    for copy in copies:
        copy.wait()

    me = lax.axis_index("dev")

    def add_column(col, total):
        s = col // 2
        h = lax.rem(col, 2)
        place = 2 * jnp.bitwise_xor(me, s + first_block) + h
        for k, g in enumerate(groups):
            for r in range(2):
                gap = g * width + 2 * me + r - place
                ahead = tables[s, COUNT_ROW, h * width + jnp.clip(gap, 0, width - 1)]
                value = jnp.where((gap >= 0) & (gap < width), ahead, 0.0)
                if g < 1:
                    behind = tables[
                        blocks + 1 + g, COUNT_ROW, r * width + jnp.clip(-gap, 0, width - 1)
                    ]
                    value = jnp.where((gap < 0) & (gap > -width), behind, value)
                plan[total] = col * n_rows + 2 * k + r
                factor[total] = value
                total = total + jnp.where(value > 0.0, 1, 0)
        return total

    live = lax.fori_loop(0, 2 * blocks, add_column, jnp.int32(0))
    for k in range(2):
        plan[live + k] = 0
        factor[live + k] = 0.0

    def build(tile, hi_ref, lo_ref):
        entry = plan[tile]
        col = entry // n_rows
        row = lax.rem(entry, n_rows)
        far = [row_points[row, k : k + 1, :] for k in range(3)]
        for at in range(0, BLOCK, STRIP):
            near = [across[col, at : at + STRIP, k : k + 1] for k in range(3)]
            for part, first in zip(wave(near, far), (0, BLOCK)):
                hi = part.astype(jnp.bfloat16)
                hi_ref[first + at : first + at + STRIP, :] = hi
                lo_ref[first + at : first + at + STRIP, :] = (
                    part - hi.astype(jnp.float32)
                ).astype(jnp.bfloat16)

    def apply(tile, hi_ref, lo_ref):
        entry = plan[tile]
        col = entry // n_rows
        row = lax.rem(entry, n_rows)
        top = jnp.dot(left[col], hi_ref[...], preferred_element_type=jnp.float32)
        rest = jnp.dot(left[col, 0:base], lo_ref[...], preferred_element_type=jnp.float32)
        acc[row] += factor[tile] * (top[:base] + top[base:] + rest)

    @pl.when(live > 0)
    def _():
        build(0, hi_a, lo_a)

        def pair(i, carry):
            apply(2 * i, hi_a, lo_a)
            build(2 * i + 1, hi_b, lo_b)
            apply(2 * i + 1, hi_b, lo_b)
            build(2 * i + 2, hi_a, lo_a)
            return carry

        lax.fori_loop(0, (live + 1) // 2, pair, 0)

    for k in range(len(groups)):
        for r in range(2):
            out[k, :, r * BLOCK : (r + 1) * BLOCK] = acc[2 * k + r]


def near_part(groups, first_block, cols, points, width, start=None):
    blocks = len(cols)
    rows, own = cols[0].shape
    base = rows - EXTRA
    lanes = -(-2 * width // 128) * 128
    n_rows = 2 * len(groups)
    kernel = functools.partial(
        near_kernel, groups, first_block, blocks, width, start is not None
    )
    args = list(cols) + list(points) + ([] if start is None else [start])
    tile = pltpu.VMEM((2 * BLOCK, BLOCK), jnp.bfloat16)
    tiles = blocks * 2 * n_rows
    return pl.pallas_call(
        kernel,
        out_shape=jax.ShapeDtypeStruct((len(groups), base, own), jnp.float32),
        in_specs=[pl.BlockSpec(memory_space=pltpu.VMEM)] * len(args),
        out_specs=pl.BlockSpec(memory_space=pltpu.VMEM),
        scratch_shapes=[
            pltpu.VMEM((2 * blocks, 2 * base, 2 * BLOCK), jnp.bfloat16),
            pltpu.VMEM((2 * blocks, BLOCK, 128), jnp.float32),
            pltpu.VMEM((n_rows, EXTRA, BLOCK), jnp.float32),
            tile,
            tile,
            tile,
            tile,
            pltpu.VMEM((n_rows, base, BLOCK), jnp.float32),
            pltpu.SMEM((blocks + 2, EXTRA, lanes), jnp.float32),
            pltpu.SMEM((tiles + 8,), jnp.int32),
            pltpu.SMEM((tiles + 8,), jnp.float32),
            pltpu.SemaphoreType.DMA((blocks + 2,)),
        ],
        compiler_params=pltpu.CompilerParams(vmem_limit_bytes=VMEM_LIMIT),
        cost_estimate=pl.CostEstimate(
            flops=tiles * 6 * 4 * base * BLOCK * BLOCK // 2,
            bytes_accessed=4 * rows * own * (blocks + 3),
            transcendentals=tiles * BLOCK * BLOCK,
        ),
    )(*args)


def shifted(value, axis, steps):
    count = lax.axis_size(axis)
    first, last = max(0, -steps), min(count, count - steps)
    return lax.ppermute(value, axis, [(i, i + steps) for i in range(first, last)])


def swapped(value, axis, mask):
    return lax.ppermute(value, axis, [(i, i ^ mask) for i in range(lax.axis_size(axis))])


def body(drive, coords, rule_index, rule_weight, pair_cols, pair_count):
    n_dev = lax.axis_size("dev")
    patterns, own = drive.shape[1:]
    width = n_dev * (own // BLOCK)
    vmem, smem = (pl.BlockSpec(memory_space=m) for m in (pltpu.VMEM, pltpu.SMEM))
    payload = pl.pallas_call(
        functools.partial(pack_kernel, width),
        out_shape=jax.ShapeDtypeStruct((2 * patterns + EXTRA, own), jnp.float32),
        in_specs=[vmem, vmem, vmem, smem, smem, smem],
        out_specs=vmem,
    )(drive, coords, rule_index[None, :], rule_weight, pair_cols, pair_count)
    base = 2 * patterns
    mine = payload[base:]
    points = (shifted(mine, "band", 1), mine, shifted(mine, "band", -1))
    same = {0: payload}
    for mask in range(2, n_dev, 2):
        same[mask] = swapped(payload, "dev", mask)
    held = dict(same)
    for mask, value in same.items():
        held[mask + 1] = swapped(value, "dev", 1)
    first = near_part((-1, 0, 1), 0, [held[0], held[1]], points, width)
    later = [held[mask] for mask in range(2, n_dev)]
    edges = near_part((-1, 1), 2, later, points, width, first[0::2])
    from_after = shifted(edges[0], "band", -1)
    from_before = shifted(edges[1], "band", 1)
    middle = near_part((0,), 2, later, points, width, first[1:2])
    total = (middle[0] + from_after + from_before) * mine[WEIGHT_ROW]
    return total.reshape(drive.shape)


def solution(mesh):
    spread = ("band", "dev")
    in_specs = (
        P(None, None, spread),
        P(None, spread),
        P(spread),
        P(),
        P(spread),
        P(spread),
    )
    out_specs = P(None, None, spread)
    return jax.shard_map(body, mesh=mesh, in_specs=in_specs, out_specs=out_specs, check_vma=False)
```

```python
import functools
import math

import jax
import jax.numpy as jnp
from jax import lax
from jax.experimental import pallas as pl
from jax.experimental.pallas import tpu as pltpu
from jax.sharding import PartitionSpec as P

BLOCK = 256
STRIP = 16
VMEM_LIMIT = 48 * 1024 * 1024

wave_number = 25.0
smoothing = 0.05
per_unit = wave_number / (2.0 * math.pi)
core_sq = (smoothing * per_unit) ** 2
amplitude = per_unit / (4.0 * math.pi)
SINE = (4.4428679, -7.30744342, 3.59478806, -0.78437397)
COSINE = (1.4142135, -6.97885099, 5.73946117, -1.88356297, 0.31069815)

COUNT_ROW = 3
WEIGHT_ROW = 4
EXTRA = 8


def horner(z, terms):
    value = z * terms[-1] + terms[-2]
    for term in terms[-3::-1]:
        value = value * z + term
    return value


def wave(near, far):
    square = None
    for a, b in zip(near, far):
        gap = a - b
        gap = gap * gap
        square = gap + core_sq if square is None else square + gap
    inverse = lax.rsqrt(square)
    turns = square * inverse
    part = turns - jnp.round(turns)
    z = part * part
    s = horner(z, SINE) * part
    scaled = inverse * s
    return inverse - scaled * s, scaled * horner(z, COSINE)


def pack_kernel(width, drive, coords, rules, rule_weight, pair_cols, pair_count, out):
    patterns = drive.shape[1]
    first_row = (lax.axis_index("band") * lax.axis_size("dev") + lax.axis_index("dev")) * 2
    weight = jnp.zeros(rules.shape, jnp.float32)
    for rule in range(rule_weight.shape[0]):
        weight = jnp.where(rules[...] == rule, rule_weight[rule], weight)
    scale = weight * amplitude
    out[0:patterns, :] = drive[0] * scale
    out[patterns : 2 * patterns, :] = drive[1] * scale
    lanes = lax.broadcasted_iota(jnp.int32, rules.shape, 1)

    def count(slot, totals):
        odd = lax.rem(slot, 2)
        place = pair_cols[slot] - first_row - odd + odd * width
        return totals + jnp.where(lanes == place, 1.0, 0.0)

    counts = lax.fori_loop(0, pair_count[0], count, jnp.zeros(rules.shape, jnp.float32))
    base = 2 * patterns
    out[base : base + EXTRA, :] = jnp.zeros((EXTRA, out.shape[1]), jnp.float32)
    out[base : base + 3, :] = coords[...] * per_unit
    out[base + COUNT_ROW : base + COUNT_ROW + 1, :] = counts
    out[base + WEIGHT_ROW : base + WEIGHT_ROW + 1, :] = weight


def near_kernel(groups, first_block, blocks, width, has_start, *refs):
    cols = refs[:blocks]
    points = refs[blocks : blocks + 3]
    refs = refs[blocks + 3 :]
    start, refs = (refs[0], refs[1:]) if has_start else (None, refs)
    out, left, across, row_points, hi_a, lo_a, hi_b, lo_b, acc, tables, plan, factor, sem = refs
    base = cols[0].shape[0] - EXTRA
    half = base // 2
    lanes = tables.shape[2]
    n_rows = 2 * len(groups)
    copies = [
        pltpu.make_async_copy(
            cols[s].at[base : base + EXTRA, 0:lanes], tables.at[s], sem.at[s]
        )
        for s in range(blocks)
    ] + [
        pltpu.make_async_copy(
            points[g].at[:, 0:lanes], tables.at[blocks + g], sem.at[blocks + g]
        )
        for g in range(2)
    ]
    for copy in copies:
        copy.start()
    for s in range(blocks):
        for h in range(2):
            span = slice(h * BLOCK, (h + 1) * BLOCK)
            x = cols[s][0:base, span]
            wide = jnp.concatenate([x, jnp.concatenate([-x[half:], x[:half]], 0)], 1)
            hi = wide.astype(jnp.bfloat16)
            left[2 * s + h, 0:base, :] = hi
            left[2 * s + h, base : 2 * base, :] = (wide - hi.astype(jnp.float32)).astype(
                jnp.bfloat16
            )
            across[2 * s + h, :, 0:EXTRA] = cols[s][base : base + EXTRA, span].T
    for k, g in enumerate(groups):
        for r in range(2):
            row_points[2 * k + r] = points[g + 1][:, r * BLOCK : (r + 1) * BLOCK]
            if has_start:
                acc[2 * k + r] = start[k, :, r * BLOCK : (r + 1) * BLOCK]
            else:
                acc[2 * k + r] = jnp.zeros(acc.shape[1:], jnp.float32)
    for copy in copies:
        copy.wait()

    me = lax.axis_index("dev")

    def add_column(col, total):
        s = col // 2
        h = lax.rem(col, 2)
        place = 2 * jnp.bitwise_xor(me, s + first_block) + h
        for k, g in enumerate(groups):
            for r in range(2):
                gap = g * width + 2 * me + r - place
                ahead = tables[s, COUNT_ROW, h * width + jnp.clip(gap, 0, width - 1)]
                value = jnp.where((gap >= 0) & (gap < width), ahead, 0.0)
                if g < 1:
                    behind = tables[
                        blocks + 1 + g, COUNT_ROW, r * width + jnp.clip(-gap, 0, width - 1)
                    ]
                    value = jnp.where((gap < 0) & (gap > -width), behind, value)
                plan[total] = col * n_rows + 2 * k + r
                factor[total] = value
                total = total + jnp.where(value > 0.0, 1, 0)
        return total

    live = lax.fori_loop(0, 2 * blocks, add_column, jnp.int32(0))
    for k in range(2):
        plan[live + k] = 0
        factor[live + k] = 0.0

    def build(tile, hi_ref, lo_ref):
        entry = plan[tile]
        col = entry // n_rows
        row = lax.rem(entry, n_rows)
        far = [row_points[row, k : k + 1, :] for k in range(3)]
        for at in range(0, BLOCK, STRIP):
            near = [across[col, at : at + STRIP, k : k + 1] for k in range(3)]
            for part, first in zip(wave(near, far), (0, BLOCK)):
                hi = part.astype(jnp.bfloat16)
                hi_ref[first + at : first + at + STRIP, :] = hi
                lo_ref[first + at : first + at + STRIP, :] = (
                    part - hi.astype(jnp.float32)
                ).astype(jnp.bfloat16)

    def apply(tile, hi_ref, lo_ref):
        entry = plan[tile]
        col = entry // n_rows
        row = lax.rem(entry, n_rows)
        top = jnp.dot(left[col], hi_ref[...], preferred_element_type=jnp.float32)
        rest = jnp.dot(left[col, 0:base], lo_ref[...], preferred_element_type=jnp.float32)
        acc[row] += factor[tile] * (top[:base] + top[base:] + rest)

    @pl.when(live > 0)
    def _():
        build(0, hi_a, lo_a)

        def pair(i, carry):
            apply(2 * i, hi_a, lo_a)
            build(2 * i + 1, hi_b, lo_b)
            apply(2 * i + 1, hi_b, lo_b)
            build(2 * i + 2, hi_a, lo_a)
            return carry

        lax.fori_loop(0, (live + 1) // 2, pair, 0)

    for k in range(len(groups)):
        for r in range(2):
            out[k, :, r * BLOCK : (r + 1) * BLOCK] = acc[2 * k + r]


def near_part(groups, first_block, cols, points, width, start=None):
    blocks = len(cols)
    rows, own = cols[0].shape
    base = rows - EXTRA
    lanes = -(-2 * width // 128) * 128
    n_rows = 2 * len(groups)
    kernel = functools.partial(
        near_kernel, groups, first_block, blocks, width, start is not None
    )
    args = list(cols) + list(points) + ([] if start is None else [start])
    tile = pltpu.VMEM((2 * BLOCK, BLOCK), jnp.bfloat16)
    tiles = blocks * 2 * n_rows
    return pl.pallas_call(
        kernel,
        out_shape=jax.ShapeDtypeStruct((len(groups), base, own), jnp.float32),
        in_specs=[pl.BlockSpec(memory_space=pltpu.VMEM)] * len(args),
        out_specs=pl.BlockSpec(memory_space=pltpu.VMEM),
        scratch_shapes=[
            pltpu.VMEM((2 * blocks, 2 * base, 2 * BLOCK), jnp.bfloat16),
            pltpu.VMEM((2 * blocks, BLOCK, 128), jnp.float32),
            pltpu.VMEM((n_rows, EXTRA, BLOCK), jnp.float32),
            tile,
            tile,
            tile,
            tile,
            pltpu.VMEM((n_rows, base, BLOCK), jnp.float32),
            pltpu.SMEM((blocks + 2, EXTRA, lanes), jnp.float32),
            pltpu.SMEM((tiles + 8,), jnp.int32),
            pltpu.SMEM((tiles + 8,), jnp.float32),
            pltpu.SemaphoreType.DMA((blocks + 2,)),
        ],
        compiler_params=pltpu.CompilerParams(vmem_limit_bytes=VMEM_LIMIT),
        cost_estimate=pl.CostEstimate(
            flops=tiles * 6 * 4 * base * BLOCK * BLOCK // 2,
            bytes_accessed=4 * rows * own * (blocks + 3),
            transcendentals=tiles * BLOCK * BLOCK,
        ),
    )(*args)


def shifted(value, axis, steps):
    count = lax.axis_size(axis)
    first, last = max(0, -steps), min(count, count - steps)
    return lax.ppermute(value, axis, [(i, i + steps) for i in range(first, last)])


def swapped(value, axis, mask):
    return lax.ppermute(value, axis, [(i, i ^ mask) for i in range(lax.axis_size(axis))])


def body(drive, coords, rule_index, rule_weight, pair_cols, pair_count):
    n_dev = lax.axis_size("dev")
    patterns, own = drive.shape[1:]
    width = n_dev * (own // BLOCK)
    vmem, smem = (pl.BlockSpec(memory_space=m) for m in (pltpu.VMEM, pltpu.SMEM))
    payload = pl.pallas_call(
        functools.partial(pack_kernel, width),
        out_shape=jax.ShapeDtypeStruct((2 * patterns + EXTRA, own), jnp.float32),
        in_specs=[vmem, vmem, vmem, smem, smem, smem],
        out_specs=vmem,
    )(drive, coords, rule_index[None, :], rule_weight, pair_cols, pair_count)
    base = 2 * patterns
    partner = swapped(payload, "dev", 1)
    mine, partner = lax.optimization_barrier((payload[base:], partner))
    points = (shifted(mine, "band", 1), mine, shifted(mine, "band", -1))
    same = [swapped(payload, "dev", mask) for mask in range(2, n_dev, 2)]
    held = {0: payload, 1: partner}
    first = near_part((-1, 0, 1), 0, [held[0], held[1]], points, width)
    same, first = lax.optimization_barrier((same, first))
    for mask, value in zip(range(2, n_dev, 2), same):
        held[mask] = value
        held[mask + 1] = swapped(value, "dev", 1)
    later = [held[mask] for mask in range(2, n_dev)]
    edges = near_part((-1, 1), 2, later, points, width, first[0::2])
    from_after = shifted(edges[0], "band", -1)
    from_before = shifted(edges[1], "band", 1)
    middle = near_part((0,), 2, later, points, width, first[1:2])
    total = (middle[0] + from_after + from_before) * mine[WEIGHT_ROW]
    return total.reshape(drive.shape)


def solution(mesh):
    spread = ("band", "dev")
    in_specs = (
        P(None, None, spread),
        P(None, spread),
        P(spread),
        P(),
        P(spread),
        P(spread),
    )
    out_specs = P(None, None, spread)
    return jax.shard_map(body, mesh=mesh, in_specs=in_specs, out_specs=out_specs, check_vma=False)
```

```python
import functools
import math

import jax
import jax.numpy as jnp
from jax import lax
from jax.experimental import pallas as pl
from jax.experimental.pallas import tpu as pltpu
from jax.sharding import PartitionSpec as P

BLOCK = 256
STRIP = 16
VMEM_LIMIT = 48 * 1024 * 1024

wave_number = 25.0
smoothing = 0.05
per_unit = wave_number / (2.0 * math.pi)
core_sq = (smoothing * per_unit) ** 2
amplitude = per_unit / (4.0 * math.pi)
SINE = (4.4428679, -7.30744342, 3.59478806, -0.78437397)
COSINE = (1.4142135, -6.97885099, 5.73946117, -1.88356297, 0.31069815)

COUNT_ROW = 3
WEIGHT_ROW = 4
EXTRA = 8


def horner(z, terms):
    value = z * terms[-1] + terms[-2]
    for term in terms[-3::-1]:
        value = value * z + term
    return value


def wave(near, far):
    square = None
    for a, b in zip(near, far):
        gap = a - b
        gap = gap * gap
        square = gap + core_sq if square is None else square + gap
    inverse = lax.rsqrt(square)
    turns = square * inverse
    part = turns - jnp.round(turns)
    z = part * part
    s = horner(z, SINE) * part
    scaled = inverse * s
    return inverse - scaled * s, scaled * horner(z, COSINE)


def pack_kernel(width, drive, coords, rules, rule_weight, pair_cols, pair_count, out, extra):
    patterns = drive.shape[1]
    slots = pair_cols.shape[1]
    first_row = (lax.axis_index("band") * lax.axis_size("dev") + lax.axis_index("dev")) * 2
    weight = jnp.zeros(rules.shape, jnp.float32)
    for rule in range(rule_weight.shape[1]):
        weight = jnp.where(rules[...] == rule, rule_weight[0:1, rule : rule + 1], weight)
    scale = weight * amplitude
    out[0:patterns, :] = drive[0] * scale
    out[patterns : 2 * patterns, :] = drive[1] * scale
    slot = lax.broadcasted_iota(jnp.int32, (8, slots), 1)
    odd = lax.rem(slot, 2)
    place = pair_cols[...] - first_row - odd + odd * width
    place = jnp.where(slot < pair_count[...], place, -1).T[:, 0:1]
    lanes = lax.broadcasted_iota(jnp.int32, (slots, 2 * width), 1)
    counts = jnp.sum(jnp.where(lanes == place, 1.0, 0.0), axis=0, keepdims=True)
    base = 2 * patterns
    for ref, first in ((out, base), (extra, 0)):
        ref[first : first + EXTRA, :] = jnp.zeros((EXTRA, out.shape[1]), jnp.float32)
        ref[first : first + 3, :] = coords[...] * per_unit
        ref[first + COUNT_ROW : first + COUNT_ROW + 1, 0 : 2 * width] = counts
        ref[first + WEIGHT_ROW : first + WEIGHT_ROW + 1, :] = weight


def near_kernel(spec, *refs):
    blocks, first_block, width, groups, outs = (
        spec[k] for k in ("blocks", "first_block", "width", "groups", "outs")
    )
    cols, refs = refs[:blocks], refs[blocks:]
    ready, refs = (refs[:2], refs[2:]) if spec["reuse"] else (None, refs)
    points, refs = refs[: 1 if groups == (0,) else 3], refs[1 if groups == (0,) else 3 :]
    starts, refs = (refs[: len(outs)], refs[len(outs) :]) if spec["started"] else (None, refs)
    results, refs = refs[: len(outs)], refs[len(outs) :]
    if spec["reuse"]:
        left, across = ready
    else:
        left, across, refs = refs[0], refs[1], refs[2:]
    row_points, hi_a, lo_a, hi_b, lo_b, acc, lists, tables, plan, factor, sem = refs
    even = lax.rem(lax.axis_index("band"), 2) == 0
    base = cols[0].shape[0] - EXTRA
    half = base // 2
    lanes = tables.shape[2]
    copies = [
        pltpu.make_async_copy(cols[s].at[base : base + EXTRA, 0:lanes], tables.at[s], sem.at[s])
        for s in range(blocks)
    ] + [
        pltpu.make_async_copy(points[0].at[:, 0:lanes], tables.at[blocks], sem.at[blocks])
    ]
    if 1 in groups:
        lists[...] = jnp.where(even, points[2][:, 0:lanes], points[1][:, 0:lanes])
        copies.append(
            pltpu.make_async_copy(lists, tables.at[blocks + 1], sem.at[blocks + 1])
        )
    for copy in copies:
        copy.start()
    if not spec["reuse"]:
        for s in range(blocks):
            for h in range(2):
                span = slice(h * BLOCK, (h + 1) * BLOCK)
                x = cols[s][0:base, span]
                wide = jnp.concatenate([x, jnp.concatenate([-x[half:], x[:half]], 0)], 1)
                hi = wide.astype(jnp.bfloat16)
                left[2 * s + h, 0:base, :] = hi
                left[2 * s + h, base : 2 * base, :] = (wide - hi.astype(jnp.float32)).astype(
                    jnp.bfloat16
                )
                across[2 * s + h, :, 0:EXTRA] = cols[s][base : base + EXTRA, span].T
    for k, g in enumerate(groups):
        for r in range(2):
            span = slice(r * BLOCK, (r + 1) * BLOCK)
            if g == 0:
                row_points[2 * k + r] = points[0][:, span]
            else:
                near, far = (1, 2) if g == 1 else (2, 1)
                row_points[2 * k + r] = jnp.where(even, points[near][:, span], points[far][:, span])
            if g in outs:
                if spec["started"]:
                    acc[2 * k + r] = starts[outs.index(g)][:, span]
                else:
                    acc[2 * k + r] = jnp.zeros(acc.shape[1:], jnp.float32)
    for copy in copies:
        copy.wait()

    me = lax.axis_index("dev")

    def place_of(col):
        s, h = lax.shift_right_logical(col, 1), jnp.bitwise_and(col, 1)
        return s, h, 2 * jnp.bitwise_xor(me, s + first_block) + h

    def add(total, col, row, value):
        plan[total] = col * 8 + row
        factor[total] = value
        return total + jnp.where(value > 0.0, 1, 0)

    def edge_column(col, total):
        s, h, j = place_of(col)
        for r in range(2):
            gap = 2 * me + r - j
            after = gap < 0
            line = jnp.where(after, s, blocks + 1)
            lane = jnp.where(after, h * width + gap, r * width - gap) + width
            value = tables[line, COUNT_ROW, jnp.minimum(lane, lanes - 1)]
            row = jnp.where(after, 2 * groups.index(1), 2 * groups.index(-1)) + r
            total = add(total, col, row, jnp.where(gap == 0, 0.0, value))
        return total

    def own_column(col, total):
        s, h, j = place_of(col)
        for r in range(2):
            gap = 2 * me + r - j
            ahead = gap >= 0
            line = jnp.where(ahead, s, blocks)
            lane = jnp.where(ahead, h * width + gap, r * width - gap)
            total = add(total, col, 2 * groups.index(0) + r, tables[line, COUNT_ROW, lane])
        return total

    live = jnp.int32(0)
    if 1 in groups:
        live = lax.fori_loop(0, 2 * blocks, edge_column, live, unroll=4)
    edge_tiles = live
    if 0 in groups:
        live = lax.fori_loop(0, 2 * blocks, own_column, live, unroll=4)
    cut = jnp.maximum(edge_tiles, jnp.minimum(live, spec["budget"]))
    first, end = {"all": (0, live), "head": (0, cut), "tail": (cut, live)}[spec["part"]]
    for k in range(2):
        plan[end + k] = 0
        factor[end + k] = 0.0

    def build(tile, hi_ref, lo_ref):
        entry = plan[tile]
        col = lax.shift_right_logical(entry, 3)
        row = jnp.bitwise_and(entry, 7)
        far = [row_points[row, k : k + 1, :] for k in range(3)]
        for at in range(0, BLOCK, STRIP):
            near = [across[col, at : at + STRIP, k : k + 1] for k in range(3)]
            for part, begin in zip(wave(near, far), (0, BLOCK)):
                hi = part.astype(jnp.bfloat16)
                hi_ref[begin + at : begin + at + STRIP, :] = hi
                lo_ref[begin + at : begin + at + STRIP, :] = (
                    part - hi.astype(jnp.float32)
                ).astype(jnp.bfloat16)

    def apply(tile, hi_ref, lo_ref):
        entry = plan[tile]
        col = lax.shift_right_logical(entry, 3)
        row = jnp.bitwise_and(entry, 7)
        top = jnp.dot(left[col], hi_ref[...], preferred_element_type=jnp.float32)
        rest = jnp.dot(left[col, 0:base], lo_ref[...], preferred_element_type=jnp.float32)
        acc[row] += factor[tile] * (top[:base] + top[base:] + rest)

    @pl.when(end > first)
    def _():
        build(first, hi_a, lo_a)

        def pair(i, carry):
            tile = first + 2 * i
            apply(tile, hi_a, lo_a)
            build(tile + 1, hi_b, lo_b)
            apply(tile + 1, hi_b, lo_b)
            build(tile + 2, hi_a, lo_a)
            return carry

        lax.fori_loop(0, (end - first + 1) // 2, pair, 0)

    for g, result in zip(outs, results):
        index = groups.index(g)
        if spec["part"] == "head" and g != 0:
            index = jnp.where(even, groups.index(-g), index)
        for r in range(2):
            result[:, r * BLOCK : (r + 1) * BLOCK] = acc[2 * index + r]


def near_part(cols, first_block, width, points, groups, outs, starts=None, part="all", ready=None):
    blocks = len(cols)
    rows, own = cols[0].shape
    base = rows - EXTRA
    lanes = -(-2 * width // 128) * 128
    n_rows = 2 * len(groups)
    spec = dict(
        blocks=blocks,
        first_block=first_block,
        width=width,
        groups=groups,
        outs=outs,
        part=part,
        started=starts is not None,
        reuse=ready is not None,
        budget=2 * blocks * 5 // 3,
    )
    args = list(cols) + list(ready or ()) + list(points) + list(starts or ())
    tile = pltpu.VMEM((2 * BLOCK, BLOCK), jnp.bfloat16)
    tiles = blocks * 2 * n_rows
    out_shape = [jax.ShapeDtypeStruct((base, own), jnp.float32) for _ in outs]
    shared = [
        jax.ShapeDtypeStruct((2 * blocks, 2 * base, 2 * BLOCK), jnp.bfloat16),
        jax.ShapeDtypeStruct((2 * blocks, BLOCK, 128), jnp.float32),
    ]
    held = [pltpu.VMEM(array.shape, array.dtype) for array in shared]
    if part == "head":
        out_shape, held = out_shape + shared, []
    elif ready is not None:
        held = []
    vmem = pl.BlockSpec(memory_space=pltpu.VMEM)
    return pl.pallas_call(
        functools.partial(near_kernel, spec),
        out_shape=out_shape,
        in_specs=[vmem] * len(args),
        out_specs=[vmem] * len(out_shape),
        scratch_shapes=held
        + [
            pltpu.VMEM((n_rows, EXTRA, BLOCK), jnp.float32),
            tile,
            tile,
            tile,
            tile,
            pltpu.VMEM((n_rows, base, BLOCK), jnp.float32),
            pltpu.VMEM((EXTRA, lanes), jnp.float32),
            pltpu.SMEM((blocks + 2, EXTRA, lanes), jnp.float32),
            pltpu.SMEM((tiles + 8,), jnp.int32),
            pltpu.SMEM((tiles + 8,), jnp.float32),
            pltpu.SemaphoreType.DMA((blocks + 2,)),
        ],
        compiler_params=pltpu.CompilerParams(vmem_limit_bytes=VMEM_LIMIT),
        cost_estimate=pl.CostEstimate(
            flops=tiles * 6 * 4 * base * BLOCK * BLOCK // 2,
            bytes_accessed=4 * rows * own * (blocks + 3),
            transcendentals=tiles * BLOCK * BLOCK,
        ),
    )(*args)


def paired(value, first):
    count = lax.axis_size("band")
    pairs = [(i, i + 1) for i in range(first, count - 1, 2)]
    return lax.ppermute(value, "band", pairs + [(j, i) for i, j in pairs])


def swapped(value, axis, mask):
    return lax.ppermute(value, axis, [(i, i ^ mask) for i in range(lax.axis_size(axis))])


def body(drive, coords, rule_index, rule_weight, pair_cols, pair_count):
    n_dev = lax.axis_size("dev")
    patterns, own = drive.shape[1:]
    width = n_dev * (own // BLOCK)
    vmem = pl.BlockSpec(memory_space=pltpu.VMEM)
    base = 2 * patterns
    payload, mine = pl.pallas_call(
        functools.partial(pack_kernel, width),
        out_shape=[
            jax.ShapeDtypeStruct((base + EXTRA, own), jnp.float32),
            jax.ShapeDtypeStruct((EXTRA, own), jnp.float32),
        ],
        in_specs=[vmem] * 6,
        out_specs=[vmem] * 2,
    )(
        drive,
        coords,
        rule_index[None, :],
        rule_weight[None, :],
        pair_cols[None, :],
        pair_count[None, :],
    )
    partner = swapped(payload, "dev", 1)
    others = [swapped(payload, "dev", mask) for mask in range(2, n_dev, 2)]
    chip = [payload, partner]
    (own_sum,) = near_part(chip, 0, width, [mine], (0,), (0,))
    outgoing, _ = lax.optimization_barrier((mine, partner))
    points = [paired(outgoing, 0), paired(outgoing, 1)]
    points, own_sum = lax.optimization_barrier((points, own_sum))
    points = [mine] + points
    edge_sums = near_part(chip, 0, width, points, (-1, 1), (-1, 1))
    others, edge_sums = lax.optimization_barrier((others, edge_sums))
    later = []
    for value in others:
        later += [value, swapped(value, "dev", 1)]
    first_edge, second_edge, own_sum, *ready = near_part(
        later, 2, width, points, (-1, 1, 0), (-1, 1, 0), [*edge_sums, own_sum], "head"
    )
    arrived = paired(first_edge, 0) + paired(second_edge, 1)
    (own_sum,) = near_part(
        later, 2, width, points, (-1, 1, 0), (0,), [own_sum], "tail", ready
    )
    total = (own_sum + arrived) * mine[WEIGHT_ROW]
    return total.reshape(drive.shape)


def solution(mesh):
    spread = ("band", "dev")
    in_specs = (
        P(None, None, spread),
        P(None, spread),
        P(spread),
        P(),
        P(spread),
        P(spread),
    )
    out_specs = P(None, None, spread)
    return jax.shard_map(body, mesh=mesh, in_specs=in_specs, out_specs=out_specs, check_vma=False)
```

```python
import functools
import math

import jax
import jax.numpy as jnp
from jax import lax
from jax.experimental import pallas as pl
from jax.experimental.pallas import tpu as pltpu
from jax.sharding import PartitionSpec as P

BLOCK = 256
STRIP = 16
UNROLL = 2
VMEM_LIMIT = 48 * 1024 * 1024

wave_number = 25.0
smoothing = 0.05
per_unit = wave_number / (2.0 * math.pi)
core_sq = (smoothing * per_unit) ** 2
amplitude = per_unit / (4.0 * math.pi)
TOP = tuple(term / 1.01171596 for term in (3.14155014, -3.02333093))
BOTTOM = tuple(term / 1.01171596 for term in (1.0, -4.25291808))

COUNT_ROW = 3
WEIGHT_ROW = 4
EXTRA = 8


def horner(z, terms):
    value = z * terms[-1] + terms[-2]
    for term in terms[-3::-1]:
        value = value * z + term
    return value


def wave(near, far):
    square = None
    for a, b in zip(near, far):
        gap = a - b
        gap = gap * gap
        square = gap + core_sq if square is None else square + gap
    inverse = lax.rsqrt(square)
    turns = square * inverse
    part = turns - jnp.round(turns)
    z = part * part
    top = horner(z, TOP) * part
    bottom = (z + BOTTOM[1]) * z + BOTTOM[0]
    top_sq, bottom_sq = top * top, bottom * bottom
    scaled = inverse * pl.reciprocal(top_sq + bottom_sq, approx=True)
    return (bottom_sq - top_sq) * scaled, (top * bottom) * scaled


def pack_kernel(width, drive, coords, rules, rule_weight, pair_cols, pair_count, out, extra):
    patterns = drive.shape[1]
    slots = pair_cols.shape[1]
    first_row = (lax.axis_index("band") * lax.axis_size("dev") + lax.axis_index("dev")) * 2
    weight = jnp.zeros(rules.shape, jnp.float32)
    for rule in range(rule_weight.shape[1]):
        weight = jnp.where(rules[...] == rule, rule_weight[0:1, rule : rule + 1], weight)
    scale = weight * amplitude
    out[0:patterns, :] = drive[0] * scale
    out[patterns : 2 * patterns, :] = drive[1] * scale
    slot = lax.broadcasted_iota(jnp.int32, (8, slots), 1)
    odd = lax.rem(slot, 2)
    place = pair_cols[...] - first_row - odd + odd * width
    place = jnp.where(slot < pair_count[...], place, -1).T[:, 0:1]
    lanes = lax.broadcasted_iota(jnp.int32, (slots, 2 * width), 1)
    counts = jnp.sum(jnp.where(lanes == place, 1.0, 0.0), axis=0, keepdims=True)
    base = 2 * patterns
    for ref, first in ((out, base), (extra, 0)):
        ref[first : first + EXTRA, :] = jnp.zeros((EXTRA, out.shape[1]), jnp.float32)
        ref[first : first + 3, :] = coords[...] * per_unit
        ref[first + COUNT_ROW : first + COUNT_ROW + 1, 0 : 2 * width] = counts
        ref[first + WEIGHT_ROW : first + WEIGHT_ROW + 1, :] = weight


def near_kernel(spec, names, *refs):
    ref = dict(zip(names, refs, strict=True))
    blocks, first_block, width, groups, outs, part = (
        spec[k] for k in ("blocks", "first_block", "width", "groups", "outs", "part")
    )
    left, across, acc, points = ref["left"], ref["across"], ref["acc"], ref["points"]
    plan, factor = ref["plan"], ref["factor"]
    own_points = ref["own_points"]
    even = lax.rem(lax.axis_index("band"), 2) == 0
    base = acc.shape[1]
    half = base // 2
    spans = [slice(r * BLOCK, (r + 1) * BLOCK) for r in range(2)]

    copies = []
    if part != "tail":
        tables, sem = ref["tables"], ref["sem"]
        lanes = tables.shape[2]
        sources = [ref["col", s].at[base : base + EXTRA, 0:lanes] for s in range(blocks)]
        sources.append(own_points.at[:, 0:lanes])
        if 1 in groups:
            before = ref["before"]
            before[...] = jnp.where(
                even, ref["points", 1][:, 0:lanes], ref["points", 0][:, 0:lanes]
            )
            sources.append(before)
        copies = [
            pltpu.make_async_copy(source, tables.at[k], sem.at[k])
            for k, source in enumerate(sources)
        ]
        for copy in copies:
            copy.start()
        for s in range(blocks):
            for h, span in enumerate(spans):
                x = ref["col", s][0:base, span]
                turned = jnp.concatenate([-2.0 * x[half:], 2.0 * x[:half]], 0)
                wide = jnp.concatenate([x, turned], 1)
                hi = wide.astype(jnp.bfloat16)
                left[2 * s + h, 0:base, :] = hi
                left[2 * s + h, base : 2 * base, :] = (wide - hi.astype(jnp.float32)).astype(
                    jnp.bfloat16
                )
                across[2 * s + h, :, 0:EXTRA] = ref["col", s][base : base + EXTRA, span].T
    for k, g in enumerate(groups):
        for r, span in enumerate(spans):
            if g in outs:
                if spec["started"]:
                    acc[2 * k + r] = ref["start", g][:, span]
                else:
                    acc[2 * k + r] = jnp.zeros(acc.shape[1:], jnp.float32)
            if g == 0:
                points[2 * k + r] = own_points[:, span]
            elif part != "tail":
                near, far = (0, 1) if g == 1 else (1, 0)
                points[2 * k + r] = jnp.where(
                    even, ref["points", near][:, span], ref["points", far][:, span]
                )
    for copy in copies:
        copy.wait()

    if part == "tail":
        first, end = ref["marks"][0], ref["marks"][1]
    else:
        me = lax.axis_index("dev")
        own_line, before_line = blocks, blocks + 1

        def add(total, s, h, row, value):
            plan[total + 1] = (2 * s + h) * 8 + row
            factor[total + 1] = value
            return total + jnp.where(value > 0.0, 1, 0)

        def column_tiles(total, s, edge):
            if s + first_block == 0:
                for h in range(2):
                    for r in range(2):
                        if edge and r == h:
                            continue
                        gap = r - h
                        if edge:
                            line = before_line if gap > 0 else own_line
                            lane, row = 2 * width - 1, 2 * groups.index(-1 if gap > 0 else 1) + r
                        else:
                            line, row = own_line, 2 * groups.index(0) + r
                            lane = h * width + gap if gap >= 0 else r * width - gap
                        total = add(total, s, h, row, tables[line, COUNT_ROW, lane])
                return total
            ahead = jnp.bitwise_xor(me, s + first_block) - me
            after = ahead > 0
            apart = 2 * jnp.abs(ahead)
            if edge:
                line = jnp.where(after, s, before_line)
                rows = jnp.where(after, 2 * groups.index(1), 2 * groups.index(-1))
                gap, first_is_col = width - apart, after
            else:
                line = jnp.where(after, own_line, s)
                rows = 2 * groups.index(0)
                gap, first_is_col = apart, jnp.logical_not(after)
            for h in range(2):
                for r in range(2):
                    if h == r:
                        lane = h * width + gap
                    else:
                        lane = gap + jnp.where(first_is_col, h * width + r - h, r * width + h - r)
                    total = add(total, s, h, rows + r, tables[line, COUNT_ROW, lane])
            return total

        live = jnp.int32(0)
        if 1 in groups:
            for s in range(blocks):
                live = column_tiles(live, s, True)
        edge_tiles = live
        if 0 in groups:
            for s in range(blocks):
                live = column_tiles(live, s, False)
        plan[0] = 0
        factor[0] = 0.0
        plan[live + 1] = 0
        factor[live + 1] = 0.0
        first, end = 0, live
        if part == "head":
            end = jnp.maximum(edge_tiles, live - spec["keep"])
            ref["marks"][0] = end
            ref["marks"][1] = live

    def entry_of(tile):
        entry = plan[tile + 1]
        return lax.shift_right_logical(entry, 3), jnp.bitwise_and(entry, 7)

    def spread(tile, near_ref):
        col, _ = entry_of(tile)
        for at in range(0, BLOCK, STRIP):
            for k in range(3):
                near_ref[k, at : at + STRIP, :] = jnp.broadcast_to(
                    across[col, at : at + STRIP, k : k + 1], (STRIP, near_ref.shape[2])
                )

    def build(tile, hi_ref, lo_ref, near_ref):
        _, row = entry_of(tile)
        far = [points[row, k : k + 1, :] for k in range(3)]
        times = BLOCK // near_ref.shape[2]
        for at in range(0, BLOCK, STRIP):
            near = [jnp.concatenate([near_ref[k, at : at + STRIP, :]] * times, 1) for k in range(3)]
            for value, begin in zip(wave(near, far), (0, BLOCK)):
                hi = value.astype(jnp.bfloat16)
                hi_ref[begin + at : begin + at + STRIP, :] = hi
                lo_ref[begin + at : begin + at + STRIP, :] = (
                    value - hi.astype(jnp.float32)
                ).astype(jnp.bfloat16)

    def apply(tile, hi_ref, lo_ref):
        col, row = entry_of(tile)
        top = jnp.dot(left[col], hi_ref[...], preferred_element_type=jnp.float32)
        rest = jnp.dot(left[col, 0:base], lo_ref[...], preferred_element_type=jnp.float32)
        acc[row] += factor[tile + 1] * (top[:base] + top[base:] + rest)

    slots = [[ref[kind, k] for kind in ("hi", "lo", "near")] for k in range(2)]

    @pl.when(end > first)
    def _():
        for array in slots[1][:2]:
            array[...] = jnp.zeros(array.shape, array.dtype)
        spread(first, slots[0][2])

        def several(i, carry):
            for k in range(UNROLL):
                tile = first + UNROLL * i + k
                here, there = slots[k % 2], slots[(k + 1) % 2]
                build(tile, *here)
                apply(tile - 1, *there[:2])
                spread(tile + 1, there[2])
            return carry

        count = end - first
        lax.fori_loop(0, count // UNROLL, several, 0)
        done = first + count // UNROLL * UNROLL
        if UNROLL > 2:

            def pair(i, carry):
                for k in range(2):
                    tile = done + 2 * i + k
                    here, there = slots[k % 2], slots[(k + 1) % 2]
                    build(tile, *here)
                    apply(tile - 1, *there[:2])
                    spread(tile + 1, there[2])
                return carry

            lax.fori_loop(0, lax.shift_right_logical(end - done, 1), pair, 0)
        odd = jnp.bitwise_and(count, 1) == 1

        @pl.when(odd)
        def _():
            build(end - 1, *slots[0])
            apply(end - 2, *slots[1][:2])
            apply(end - 1, *slots[0][:2])

        @pl.when(jnp.logical_not(odd))
        def _():
            apply(end - 1, *slots[1][:2])

    for g in outs:
        index = groups.index(g)
        if part == "head" and g != 0:
            index = jnp.where(even, groups.index(-g), index)
        for r, span in enumerate(spans):
            ref["sum", g][:, span] = acc[2 * index + r]


def near_part(part, cols, first_block, width, mine, points, groups, outs, starts, ready=None):
    if ready is None:
        blocks = len(cols)
    else:
        blocks = ready["left"].shape[0] // 2
    base, own = (starts or cols)[0].shape
    if not starts:
        base -= EXTRA
    lanes = -(-2 * width // 128) * 128
    n_rows = 2 * len(groups)
    tiles = blocks * 2 * n_rows
    vmem, smem = (pl.BlockSpec(memory_space=m) for m in (pltpu.VMEM, pltpu.SMEM))
    shared = {
        "left": ((2 * blocks, 2 * base, 2 * BLOCK), jnp.bfloat16, pltpu.VMEM),
        "across": ((2 * blocks, BLOCK, 128), jnp.float32, pltpu.VMEM),
        "plan": ((tiles + 8,), jnp.int32, pltpu.SMEM),
        "factor": ((tiles + 8,), jnp.float32, pltpu.SMEM),
    }
    marks = {"marks": ((2,), jnp.int32, pltpu.SMEM)}
    args, outputs, scratch = {}, {}, {}
    args["own_points"] = (mine, vmem)
    for k, value in enumerate(points):
        args["points", k] = (value, vmem)
    for s, value in enumerate(cols):
        args["col", s] = (value, vmem)
    for g, value in zip(outs, starts):
        args["start", g] = (value, vmem)
    for g in outs:
        outputs["sum", g] = ((base, own), jnp.float32, pltpu.VMEM)
    if part == "head":
        outputs |= shared | marks
    elif part == "tail":
        for name, (_, _, memory) in (shared | marks).items():
            args[name] = (ready[name], vmem if memory == pltpu.VMEM else smem)
    else:
        scratch |= shared
    for k in range(2):
        for kind in ("hi", "lo"):
            scratch[kind, k] = ((2 * BLOCK, BLOCK), jnp.bfloat16, pltpu.VMEM)
        scratch["near", k] = ((3, BLOCK, 128), jnp.float32, pltpu.VMEM)
    scratch["points"] = ((n_rows, EXTRA, BLOCK), jnp.float32, pltpu.VMEM)
    scratch["acc"] = ((n_rows, base, BLOCK), jnp.float32, pltpu.VMEM)
    if part != "tail":
        scratch["before"] = ((EXTRA, lanes), jnp.float32, pltpu.VMEM)
        scratch["tables"] = ((blocks + 2, EXTRA, lanes), jnp.float32, pltpu.SMEM)
    scratch_shapes = [memory(shape, dtype) for shape, dtype, memory in scratch.values()]
    names = [*args, *outputs, *scratch]
    if part != "tail":
        scratch_shapes.append(pltpu.SemaphoreType.DMA((blocks + 2,)))
        names.append("sem")
    spec = dict(
        blocks=blocks,
        first_block=first_block,
        width=width,
        groups=groups,
        outs=outs,
        part=part,
        started=bool(starts),
        keep=3 * blocks,
    )
    results = pl.pallas_call(
        functools.partial(near_kernel, spec, names),
        out_shape=[jax.ShapeDtypeStruct(shape, dtype) for shape, dtype, _ in outputs.values()],
        in_specs=[place for _, place in args.values()],
        out_specs=[vmem if memory == pltpu.VMEM else smem for _, _, memory in outputs.values()],
        scratch_shapes=scratch_shapes,
        compiler_params=pltpu.CompilerParams(vmem_limit_bytes=VMEM_LIMIT),
        cost_estimate=pl.CostEstimate(
            flops=tiles * 6 * 4 * base * BLOCK * BLOCK // 2,
            bytes_accessed=4 * base * own * (blocks + 3),
            transcendentals=tiles * BLOCK * BLOCK,
        ),
    )(*(value for value, _ in args.values()))
    return dict(zip(outputs, results, strict=True))


def paired(value, first):
    count = lax.axis_size("band")
    pairs = [(i, i + 1) for i in range(first, count - 1, 2)]
    return lax.ppermute(value, "band", pairs + [(j, i) for i, j in pairs])


def swapped(value, axis, mask):
    return lax.ppermute(value, axis, [(i, i ^ mask) for i in range(lax.axis_size(axis))])


def body(drive, coords, rule_index, rule_weight, pair_cols, pair_count):
    n_dev = lax.axis_size("dev")
    patterns, own = drive.shape[1:]
    width = n_dev * (own // BLOCK)
    vmem = pl.BlockSpec(memory_space=pltpu.VMEM)
    base = 2 * patterns
    payload, mine = pl.pallas_call(
        functools.partial(pack_kernel, width),
        out_shape=[
            pltpu.VMEM((base + EXTRA, own), jnp.float32),
            pltpu.VMEM((EXTRA, own), jnp.float32),
        ],
        in_specs=[vmem] * 6,
        out_specs=[vmem] * 2,
    )(
        drive,
        coords,
        rule_index[None, :],
        rule_weight[None, :],
        pair_cols[None, :],
        pair_count[None, :],
    )
    partner = swapped(payload, "dev", 1)
    others = [swapped(payload, "dev", mask) for mask in range(2, n_dev, 2)]
    chip = [payload, partner]
    own_sum = near_part("all", chip, 0, width, mine, [], (0,), (0,), [])["sum", 0]
    outgoing, _ = lax.optimization_barrier((mine, partner))
    points = [paired(outgoing, 0), paired(outgoing, 1)]
    points, own_sum = lax.optimization_barrier((points, own_sum))
    edges = near_part("all", chip, 0, width, mine, points, (-1, 1), (-1, 1), [])
    edges = [edges["sum", -1], edges["sum", 1]]
    others, edges = lax.optimization_barrier((others, edges))
    later = []
    for value in others:
        later += [value, swapped(value, "dev", 1)]
    groups = (-1, 1, 0)
    head = near_part("head", later, 2, width, mine, points, groups, groups, [*edges, own_sum])
    arrived = paired(head["sum", -1], 0) + paired(head["sum", 1], 1)
    tail = near_part("tail", [], 2, width, mine, [], groups, (0,), [head["sum", 0]], head)
    total = (tail["sum", 0] + arrived) * mine[WEIGHT_ROW]
    return total.reshape(drive.shape)


def solution(mesh):
    spread = ("band", "dev")
    in_specs = (
        P(None, None, spread),
        P(None, spread),
        P(spread),
        P(),
        P(spread),
        P(spread),
    )
    out_specs = P(None, None, spread)
    return jax.shard_map(body, mesh=mesh, in_specs=in_specs, out_specs=out_specs, check_vma=False)
```

```python
import functools
import math

import jax
import jax.numpy as jnp
from jax import lax
from jax.experimental import pallas as pl
from jax.experimental.pallas import tpu as pltpu
from jax.sharding import PartitionSpec as P

BLOCK = 256
STRIP = 16
UNROLL = 2
FILL = 16
FILL_LAST = 17
VMEM_LIMIT = 48 * 1024 * 1024

wave_number = 25.0
smoothing = 0.05
per_unit = wave_number / (2.0 * math.pi)
core_sq = (smoothing * per_unit) ** 2
amplitude = per_unit / (4.0 * math.pi)
TOP = tuple(term / 1.01171596 for term in (3.14155014, -3.02333093))
BOTTOM = tuple(term / 1.01171596 for term in (1.0, -4.25291808))

COUNT_ROW = 3
WEIGHT_ROW = 4
EXTRA = 8


def horner(z, terms):
    value = z * terms[-1] + terms[-2]
    for term in terms[-3::-1]:
        value = value * z + term
    return value


def wave(near, far):
    square = None
    for a, b in zip(near, far):
        gap = a - b
        gap = gap * gap
        square = gap + core_sq if square is None else square + gap
    inverse = lax.rsqrt(square)
    turns = square * inverse
    part = turns - jnp.round(turns)
    z = part * part
    top = horner(z, TOP) * part
    bottom = (z + BOTTOM[1]) * z + BOTTOM[0]
    top_sq, bottom_sq = top * top, bottom * bottom
    scaled = inverse * pl.reciprocal(top_sq + bottom_sq, approx=True)
    return (bottom_sq - top_sq) * scaled, (top * bottom) * scaled


def pack_kernel(width, drive, coords, rules, rule_weight, pair_cols, pair_count, out, extra):
    patterns = drive.shape[1]
    slots = pair_cols.shape[1]
    first_row = (lax.axis_index("band") * lax.axis_size("dev") + lax.axis_index("dev")) * 2
    weight = jnp.zeros(rules.shape, jnp.float32)
    for rule in range(rule_weight.shape[1]):
        weight = jnp.where(rules[...] == rule, rule_weight[0:1, rule : rule + 1], weight)
    scale = weight * amplitude
    out[0:patterns, :] = drive[0] * scale
    out[patterns : 2 * patterns, :] = drive[1] * scale
    slot = lax.broadcasted_iota(jnp.int32, (8, slots), 1)
    odd = lax.rem(slot, 2)
    place = pair_cols[...] - first_row - odd + odd * width
    place = jnp.where(slot < pair_count[...], place, -1).T[:, 0:1]
    lanes = lax.broadcasted_iota(jnp.int32, (slots, 2 * width), 1)
    counts = jnp.sum(jnp.where(lanes == place, 1.0, 0.0), axis=0, keepdims=True)
    base = 2 * patterns
    for ref, first in ((out, base), (extra, 0)):
        ref[first : first + EXTRA, :] = jnp.zeros((EXTRA, out.shape[1]), jnp.float32)
        ref[first : first + 3, :] = coords[...] * per_unit
        ref[first + COUNT_ROW : first + COUNT_ROW + 1, 0 : 2 * width] = counts
        ref[first + WEIGHT_ROW : first + WEIGHT_ROW + 1, :] = weight


def near_kernel(spec, names, *refs):
    ref = dict(zip(names, refs, strict=True))
    blocks, first_block, width, groups, outs, part = (
        spec[k] for k in ("blocks", "first_block", "width", "groups", "outs", "part")
    )
    left, across, acc, points = ref["left"], ref["across"], ref["acc"], ref["points"]
    plan, factor = ref["plan"], ref["factor"]
    own_points = ref["own_points"]
    even = lax.rem(lax.axis_index("band"), 2) == 0
    base = acc.shape[1]
    half = base // 2
    spans = [slice(r * BLOCK, (r + 1) * BLOCK) for r in range(2)]

    copies = []
    if part != "tail":
        tables, sem = ref["tables"], ref["sem"]
        lanes = tables.shape[2]
        sources = [ref["col", s].at[base : base + EXTRA, 0:lanes] for s in range(blocks)]
        sources.append(own_points.at[:, 0:lanes])
        if 1 in groups:
            before = ref["before"]
            before[...] = jnp.where(
                even, ref["points", 1][:, 0:lanes], ref["points", 0][:, 0:lanes]
            )
            sources.append(before)
        copies = [
            pltpu.make_async_copy(source, tables.at[k], sem.at[k])
            for k, source in enumerate(sources)
        ]
        for copy in copies:
            copy.start()
        for s in range(blocks):
            for h, span in enumerate(spans):
                x = ref["col", s][0:base, span]
                turned = jnp.concatenate([-2.0 * x[half:], 2.0 * x[:half]], 0)
                wide = jnp.concatenate([x, turned], 1)
                hi = wide.astype(jnp.bfloat16)
                left[2 * s + h, 0:base, :] = hi
                left[2 * s + h, base : 2 * base, :] = (wide - hi.astype(jnp.float32)).astype(
                    jnp.bfloat16
                )
                across[2 * s + h, :, 0:EXTRA] = ref["col", s][base : base + EXTRA, span].T
    for k, g in enumerate(groups):
        for r, span in enumerate(spans):
            if g in outs:
                if ("start", g) in ref:
                    acc[2 * k + r] = ref["start", g][:, span]
                else:
                    acc[2 * k + r] = jnp.zeros(acc.shape[1:], jnp.float32)
            if g == 0:
                points[2 * k + r] = own_points[:, span]
            elif part != "tail":
                near, far = (0, 1) if g == 1 else (1, 0)
                points[2 * k + r] = jnp.where(
                    even, ref["points", near][:, span], ref["points", far][:, span]
                )
    for copy in copies:
        copy.wait()

    if part == "tail":
        first, end = ref["marks"][0], ref["marks"][1]
    else:
        me = lax.axis_index("dev")
        own_line, before_line = blocks, blocks + 1

        def add(total, s, h, row, value):
            plan[total + 1] = (2 * s + h) * 8 + row
            factor[total + 1] = value
            return total + jnp.where(value > 0.0, 1, 0)

        def column_tiles(total, s, edge):
            if s + first_block == 0:
                for h in range(2):
                    for r in range(2):
                        if edge and r == h:
                            continue
                        gap = r - h
                        if edge:
                            line = before_line if gap > 0 else own_line
                            lane, row = 2 * width - 1, 2 * groups.index(-1 if gap > 0 else 1) + r
                        else:
                            line, row = own_line, 2 * groups.index(0) + r
                            lane = h * width + gap if gap >= 0 else r * width - gap
                        total = add(total, s, h, row, tables[line, COUNT_ROW, lane])
                return total
            ahead = jnp.bitwise_xor(me, s + first_block) - me
            after = ahead > 0
            apart = 2 * jnp.abs(ahead)
            if edge:
                line = jnp.where(after, s, before_line)
                rows = jnp.where(after, 2 * groups.index(1), 2 * groups.index(-1))
                gap, first_is_col = width - apart, after
            else:
                line = jnp.where(after, own_line, s)
                rows = 2 * groups.index(0)
                gap, first_is_col = apart, jnp.logical_not(after)
            for h in range(2):
                for r in range(2):
                    if h == r:
                        lane = h * width + gap
                    else:
                        lane = gap + jnp.where(first_is_col, h * width + r - h, r * width + h - r)
                    total = add(total, s, h, rows + r, tables[line, COUNT_ROW, lane])
            return total

        live = jnp.int32(0)
        if 1 in groups:
            for s in range(blocks):
                live = column_tiles(live, s, True)
        edge_tiles = live
        if 0 in groups:
            for s in range(spec["own_done"], blocks):
                live = column_tiles(live, s, False)
        plan[0] = 0
        factor[0] = 0.0
        plan[live + 1] = 0
        factor[live + 1] = 0.0
        first, end = 0, live
        if part == "head":
            band, bands = lax.axis_index("band"), lax.axis_size("band")
            last = (band == 0) | (band == bands - 1)
            fill = jnp.where(last, spec["fill_last"], spec["fill"])
            end = jnp.maximum(jnp.minimum(live, fill), live - spec["keep"])
            end = jnp.maximum(edge_tiles, end)
            ref["marks"][0] = end
            ref["marks"][1] = live

    def entry_of(tile):
        entry = plan[tile + 1]
        return lax.shift_right_logical(entry, 3), jnp.bitwise_and(entry, 7)

    def spread(tile, near_ref):
        col, _ = entry_of(tile)
        for at in range(0, BLOCK, STRIP):
            for k in range(3):
                near_ref[k, at : at + STRIP, :] = jnp.broadcast_to(
                    across[col, at : at + STRIP, k : k + 1], (STRIP, near_ref.shape[2])
                )

    def build(tile, hi_ref, lo_ref, near_ref):
        _, row = entry_of(tile)
        far = [points[row, k : k + 1, :] for k in range(3)]
        times = BLOCK // near_ref.shape[2]
        for at in range(0, BLOCK, STRIP):
            near = [jnp.concatenate([near_ref[k, at : at + STRIP, :]] * times, 1) for k in range(3)]
            for value, begin in zip(wave(near, far), (0, BLOCK)):
                hi = value.astype(jnp.bfloat16)
                hi_ref[begin + at : begin + at + STRIP, :] = hi
                lo_ref[begin + at : begin + at + STRIP, :] = (
                    value - hi.astype(jnp.float32)
                ).astype(jnp.bfloat16)

    def apply(tile, hi_ref, lo_ref):
        col, row = entry_of(tile)
        top = jnp.dot(left[col], hi_ref[...], preferred_element_type=jnp.float32)
        rest = jnp.dot(left[col, 0:base], lo_ref[...], preferred_element_type=jnp.float32)
        acc[row] += factor[tile + 1] * (top[:base] + top[base:] + rest)

    slots = [[ref[kind, k] for kind in ("hi", "lo", "near")] for k in range(2)]

    @pl.when(end > first)
    def _():
        for array in slots[1][:2]:
            array[...] = jnp.zeros(array.shape, array.dtype)
        spread(first, slots[0][2])

        def several(i, carry):
            for k in range(UNROLL):
                tile = first + UNROLL * i + k
                here, there = slots[k % 2], slots[(k + 1) % 2]
                build(tile, *here)
                apply(tile - 1, *there[:2])
                spread(tile + 1, there[2])
            return carry

        count = end - first
        lax.fori_loop(0, count // UNROLL, several, 0)
        done = first + count // UNROLL * UNROLL
        if UNROLL > 2:

            def pair(i, carry):
                for k in range(2):
                    tile = done + 2 * i + k
                    here, there = slots[k % 2], slots[(k + 1) % 2]
                    build(tile, *here)
                    apply(tile - 1, *there[:2])
                    spread(tile + 1, there[2])
                return carry

            lax.fori_loop(0, lax.shift_right_logical(end - done, 1), pair, 0)
        odd = jnp.bitwise_and(count, 1) == 1

        @pl.when(odd)
        def _():
            build(end - 1, *slots[0])
            apply(end - 2, *slots[1][:2])
            apply(end - 1, *slots[0][:2])

        @pl.when(jnp.logical_not(odd))
        def _():
            apply(end - 1, *slots[1][:2])

    for g in outs:
        index = groups.index(g)
        if part == "head" and g != 0:
            index = jnp.where(even, groups.index(-g), index)
        for r, span in enumerate(spans):
            ref["sum", g][:, span] = acc[2 * index + r]


def near_part(
    part, cols, first_block, width, mine, points, groups, outs, starts, ready=None, own_done=0
):
    if ready is None:
        blocks = len(cols)
    else:
        blocks = ready["left"].shape[0] // 2
    if cols:
        base, own = cols[0].shape[0] - EXTRA, cols[0].shape[1]
    else:
        base, own = starts[0].shape
    lanes = -(-2 * width // 128) * 128
    n_rows = 2 * len(groups)
    tiles = blocks * 2 * n_rows
    vmem, smem = (pl.BlockSpec(memory_space=m) for m in (pltpu.VMEM, pltpu.SMEM))
    shared = {
        "left": ((2 * blocks, 2 * base, 2 * BLOCK), jnp.bfloat16, pltpu.VMEM),
        "across": ((2 * blocks, BLOCK, 128), jnp.float32, pltpu.VMEM),
        "plan": ((tiles + 8,), jnp.int32, pltpu.SMEM),
        "factor": ((tiles + 8,), jnp.float32, pltpu.SMEM),
    }
    marks = {"marks": ((2,), jnp.int32, pltpu.SMEM)}
    args, outputs, scratch = {}, {}, {}
    args["own_points"] = (mine, vmem)
    for k, value in enumerate(points):
        args["points", k] = (value, vmem)
    for s, value in enumerate(cols):
        args["col", s] = (value, vmem)
    for g, value in starts.items():
        args["start", g] = (value, vmem)
    for g in outs:
        outputs["sum", g] = ((base, own), jnp.float32, pltpu.VMEM)
    if part == "head":
        outputs |= shared | marks
    elif part == "tail":
        for name, (_, _, memory) in (shared | marks).items():
            args[name] = (ready[name], vmem if memory == pltpu.VMEM else smem)
    else:
        scratch |= shared
    for k in range(2):
        for kind in ("hi", "lo"):
            scratch[kind, k] = ((2 * BLOCK, BLOCK), jnp.bfloat16, pltpu.VMEM)
        scratch["near", k] = ((3, BLOCK, 128), jnp.float32, pltpu.VMEM)
    scratch["points"] = ((n_rows, EXTRA, BLOCK), jnp.float32, pltpu.VMEM)
    scratch["acc"] = ((n_rows, base, BLOCK), jnp.float32, pltpu.VMEM)
    if part != "tail":
        scratch["before"] = ((EXTRA, lanes), jnp.float32, pltpu.VMEM)
        scratch["tables"] = ((blocks + 2, EXTRA, lanes), jnp.float32, pltpu.SMEM)
    scratch_shapes = [memory(shape, dtype) for shape, dtype, memory in scratch.values()]
    names = [*args, *outputs, *scratch]
    if part != "tail":
        scratch_shapes.append(pltpu.SemaphoreType.DMA((blocks + 2,)))
        names.append("sem")
    spec = dict(
        blocks=blocks,
        first_block=first_block,
        width=width,
        groups=groups,
        outs=outs,
        part=part,
        own_done=own_done,
        keep=13 * blocks // 5,
        fill=FILL * blocks // 5,
        fill_last=FILL_LAST * blocks // 5,
    )
    results = pl.pallas_call(
        functools.partial(near_kernel, spec, names),
        out_shape=[jax.ShapeDtypeStruct(shape, dtype) for shape, dtype, _ in outputs.values()],
        in_specs=[place for _, place in args.values()],
        out_specs=[vmem if memory == pltpu.VMEM else smem for _, _, memory in outputs.values()],
        scratch_shapes=scratch_shapes,
        compiler_params=pltpu.CompilerParams(vmem_limit_bytes=VMEM_LIMIT),
        cost_estimate=pl.CostEstimate(
            flops=tiles * 6 * 4 * base * BLOCK * BLOCK // 2,
            bytes_accessed=4 * base * own * (blocks + 3),
            transcendentals=tiles * BLOCK * BLOCK,
        ),
    )(*(value for value, _ in args.values()))
    return dict(zip(outputs, results, strict=True))


def paired(value, first):
    count = lax.axis_size("band")
    pairs = [(i, i + 1) for i in range(first, count - 1, 2)]
    return lax.ppermute(value, "band", pairs + [(j, i) for i, j in pairs])


def swapped(value, axis, mask):
    return lax.ppermute(value, axis, [(i, i ^ mask) for i in range(lax.axis_size(axis))])


def body(drive, coords, rule_index, rule_weight, pair_cols, pair_count):
    n_dev = lax.axis_size("dev")
    patterns, own = drive.shape[1:]
    width = n_dev * (own // BLOCK)
    vmem = pl.BlockSpec(memory_space=pltpu.VMEM)
    base = 2 * patterns
    payload, mine = pl.pallas_call(
        functools.partial(pack_kernel, width),
        out_shape=[
            pltpu.VMEM((base + EXTRA, own), jnp.float32),
            pltpu.VMEM((EXTRA, own), jnp.float32),
        ],
        in_specs=[vmem] * 6,
        out_specs=[vmem] * 2,
    )(
        drive,
        coords,
        rule_index[None, :],
        rule_weight[None, :],
        pair_cols[None, :],
        pair_count[None, :],
    )
    partner = swapped(payload, "dev", 1)
    others = [swapped(payload, "dev", mask) for mask in range(2, n_dev, 2)]
    chip = [payload, partner]
    own_sum = near_part("all", chip, 0, width, mine, [], (0,), (0,), {})["sum", 0]
    outgoing, _ = lax.optimization_barrier((mine, partner))
    points = [paired(outgoing, 0), paired(outgoing, 1)]
    points, own_sum = lax.optimization_barrier((points, own_sum))
    groups = (-1, 1, 0)
    cols = chip + others[:1]
    early = near_part(
        "all", cols, 0, width, mine, points, groups, groups, {0: own_sum}, own_done=2
    )
    sums = {g: early["sum", g] for g in groups}
    others, sums = lax.optimization_barrier((others, sums))
    later = [swapped(others[0], "dev", 1)]
    for value in others[1:]:
        later += [value, swapped(value, "dev", 1)]
    head = near_part("head", later, len(cols), width, mine, points, groups, groups, sums)
    arrived = paired(head["sum", 1], 1) + paired(head["sum", -1], 0)
    tail = near_part("tail", [], 2, width, mine, [], groups, (0,), {0: head["sum", 0]}, head)
    total = (tail["sum", 0] + arrived) * mine[WEIGHT_ROW]
    return total.reshape(drive.shape)


def solution(mesh):
    spread = ("band", "dev")
    in_specs = (
        P(None, None, spread),
        P(None, spread),
        P(spread),
        P(),
        P(spread),
        P(spread),
    )
    out_specs = P(None, None, spread)
    return jax.shard_map(body, mesh=mesh, in_specs=in_specs, out_specs=out_specs, check_vma=False)
```

```python
import functools
import math

import jax
import jax.numpy as jnp
from jax import lax
from jax.experimental import pallas as pl
from jax.experimental.pallas import tpu as pltpu
from jax.sharding import PartitionSpec as P

BLOCK = 256
STRIP = 16
UNROLL = 2
FILL = 16
FILL_LAST = 17
VMEM_LIMIT = 48 * 1024 * 1024

wave_number = 25.0
smoothing = 0.05
per_unit = wave_number / (2.0 * math.pi)
core_sq = (smoothing * per_unit) ** 2
amplitude = per_unit / (4.0 * math.pi)
TOP = tuple(term / 1.01171596 for term in (3.14155014, -3.02333093))
BOTTOM = tuple(term / 1.01171596 for term in (1.0, -4.25291808))

COUNT_ROW = 3
WEIGHT_ROW = 4
EXTRA = 8


def horner(z, terms):
    value = z * terms[-1] + terms[-2]
    for term in terms[-3::-1]:
        value = value * z + term
    return value


def wave(near, far):
    square = None
    for a, b in zip(near, far):
        gap = a - b
        gap = gap * gap
        square = gap + core_sq if square is None else square + gap
    inverse = lax.rsqrt(square)
    turns = square * inverse
    part = turns - jnp.round(turns)
    z = part * part
    top = horner(z, TOP) * part
    bottom = (z + BOTTOM[1]) * z + BOTTOM[0]
    top_sq, bottom_sq = top * top, bottom * bottom
    scaled = inverse * pl.reciprocal(top_sq + bottom_sq, approx=True)
    return (bottom_sq - top_sq) * scaled, (top * bottom) * scaled


def pack_kernel(width, drive, coords, rules, rule_weight, pair_cols, pair_count, out, extra):
    patterns = drive.shape[1]
    slots = pair_cols.shape[1]
    first_row = (lax.axis_index("band") * lax.axis_size("dev") + lax.axis_index("dev")) * 2
    weight = jnp.zeros(rules.shape, jnp.float32)
    for rule in range(rule_weight.shape[1]):
        weight = jnp.where(rules[...] == rule, rule_weight[0:1, rule : rule + 1], weight)
    scale = weight * amplitude
    out[0:patterns, :] = drive[0] * scale
    out[patterns : 2 * patterns, :] = drive[1] * scale
    slot = lax.broadcasted_iota(jnp.int32, (8, slots), 1)
    odd = lax.rem(slot, 2)
    place = pair_cols[...] - first_row - odd + odd * width
    place = jnp.where(slot < pair_count[...], place, -1).T[:, 0:1]
    lanes = lax.broadcasted_iota(jnp.int32, (slots, 2 * width), 1)
    counts = jnp.sum(jnp.where(lanes == place, 1.0, 0.0), axis=0, keepdims=True)
    base = 2 * patterns
    for ref, first in ((out, base), (extra, 0)):
        ref[first : first + EXTRA, :] = jnp.zeros((EXTRA, out.shape[1]), jnp.float32)
        ref[first : first + 3, :] = coords[...] * per_unit
        ref[first + COUNT_ROW : first + COUNT_ROW + 1, 0 : 2 * width] = counts
        ref[first + WEIGHT_ROW : first + WEIGHT_ROW + 1, :] = weight


def near_kernel(spec, names, *refs):
    ref = dict(zip(names, refs, strict=True))
    blocks, first_block, width, groups, outs, part = (
        spec[k] for k in ("blocks", "first_block", "width", "groups", "outs", "part")
    )
    left, across, acc, points = ref["left"], ref["across"], ref["acc"], ref["points"]
    plan, factor = ref["plan"], ref["factor"]
    own_points = ref["own_points"]
    even = lax.rem(lax.axis_index("band"), 2) == 0
    base = acc.shape[1]
    half = base // 2
    spans = [slice(r * BLOCK, (r + 1) * BLOCK) for r in range(2)]

    copies = []
    if part != "tail":
        tables, sem = ref["tables"], ref["sem"]
        lanes = tables.shape[2]
        sources = [ref["col", s].at[base : base + EXTRA, 0:lanes] for s in range(blocks)]
        sources.append(own_points.at[:, 0:lanes])
        if 1 in groups:
            before = ref["before"]
            before[...] = jnp.where(
                even, ref["points", 1][:, 0:lanes], ref["points", 0][:, 0:lanes]
            )
            sources.append(before)
        copies = [
            pltpu.make_async_copy(source, tables.at[k], sem.at[k])
            for k, source in enumerate(sources)
        ]
        for copy in copies:
            copy.start()
        for s in range(blocks):
            for h, span in enumerate(spans):
                x = ref["col", s][0:base, span]
                turned = jnp.concatenate([-2.0 * x[half:], 2.0 * x[:half]], 0)
                wide = jnp.concatenate([x, turned], 1)
                hi = wide.astype(jnp.bfloat16)
                left[2 * s + h, 0:base, :] = hi
                left[2 * s + h, base : 2 * base, :] = (wide - hi.astype(jnp.float32)).astype(
                    jnp.bfloat16
                )
        lines = [ref["col", s][base : base + EXTRA, span] for s in range(blocks) for span in spans]
        for k in range(across.shape[0]):
            some = lines[16 * k : 16 * (k + 1)]
            spare = 128 - EXTRA * len(some)
            if spare:
                some.append(jnp.zeros((spare, BLOCK), jnp.float32))
            across[k] = jnp.concatenate(some, 0).T
    for k, g in enumerate(groups):
        for r, span in enumerate(spans):
            if g in outs:
                if ("start", g) in ref:
                    acc[2 * k + r] = ref["start", g][:, span]
                else:
                    acc[2 * k + r] = jnp.zeros(acc.shape[1:], jnp.float32)
            if g == 0:
                points[2 * k + r] = own_points[:, span]
            elif part != "tail":
                near, far = (0, 1) if g == 1 else (1, 0)
                points[2 * k + r] = jnp.where(
                    even, ref["points", near][:, span], ref["points", far][:, span]
                )
    for copy in copies:
        copy.wait()

    if part == "tail":
        first, end = ref["marks"][0], ref["marks"][1]
    else:
        me = lax.axis_index("dev")
        own_line, before_line = blocks, blocks + 1

        def add(total, s, h, row, value):
            plan[total + 1] = (2 * s + h) * 8 + row
            factor[total + 1] = value
            return total + jnp.where(value > 0.0, 1, 0)

        def column_tiles(total, s, edge):
            if s + first_block == 0:
                for h in range(2):
                    for r in range(2):
                        if edge and r == h:
                            continue
                        gap = r - h
                        if edge:
                            line = before_line if gap > 0 else own_line
                            lane, row = 2 * width - 1, 2 * groups.index(-1 if gap > 0 else 1) + r
                        else:
                            line, row = own_line, 2 * groups.index(0) + r
                            lane = h * width + gap if gap >= 0 else r * width - gap
                        total = add(total, s, h, row, tables[line, COUNT_ROW, lane])
                return total
            ahead = jnp.bitwise_xor(me, s + first_block) - me
            after = ahead > 0
            apart = 2 * jnp.abs(ahead)
            if edge:
                line = jnp.where(after, s, before_line)
                rows = jnp.where(after, 2 * groups.index(1), 2 * groups.index(-1))
                gap, first_is_col = width - apart, after
            else:
                line = jnp.where(after, own_line, s)
                rows = 2 * groups.index(0)
                gap, first_is_col = apart, jnp.logical_not(after)
            for h in range(2):
                for r in range(2):
                    if h == r:
                        lane = h * width + gap
                    else:
                        lane = gap + jnp.where(first_is_col, h * width + r - h, r * width + h - r)
                    total = add(total, s, h, rows + r, tables[line, COUNT_ROW, lane])
            return total

        live = jnp.int32(0)
        if 1 in groups:
            for s in range(blocks):
                live = column_tiles(live, s, True)
        edge_tiles = live
        if 0 in groups:
            for s in range(spec["own_done"], blocks):
                live = column_tiles(live, s, False)
        plan[0] = 0
        factor[0] = 0.0
        plan[live + 1] = 0
        factor[live + 1] = 0.0
        first, end = 0, live
        if part == "head":
            band, bands = lax.axis_index("band"), lax.axis_size("band")
            last = (band == 0) | (band == bands - 1)
            fill = jnp.where(last, spec["fill_last"], spec["fill"])
            end = jnp.maximum(jnp.minimum(live, fill), live - spec["keep"])
            end = jnp.maximum(edge_tiles, end)
            ref["marks"][0] = end
            ref["marks"][1] = live

    def entry_of(tile):
        entry = plan[tile + 1]
        return lax.shift_right_logical(entry, 3), jnp.bitwise_and(entry, 7)

    def spread(tile, near_ref):
        col, _ = entry_of(tile)
        group = lax.shift_right_logical(col, 4)
        lane = EXTRA * jnp.bitwise_and(col, 15)
        for k in range(3):
            pick = jnp.full((8, 128), lane + k, jnp.int32)
            for at in range(0, BLOCK, 8):
                near_ref[k, at : at + 8, :] = jnp.take_along_axis(
                    across[group, at : at + 8, :], pick, axis=1, mode="promise_in_bounds"
                )

    def build(tile, hi_ref, lo_ref, near_ref):
        _, row = entry_of(tile)
        far = [points[row, k : k + 1, :] for k in range(3)]
        times = BLOCK // near_ref.shape[2]
        for at in range(0, BLOCK, STRIP):
            near = [jnp.concatenate([near_ref[k, at : at + STRIP, :]] * times, 1) for k in range(3)]
            for value, begin in zip(wave(near, far), (0, BLOCK)):
                hi = value.astype(jnp.bfloat16)
                hi_ref[begin + at : begin + at + STRIP, :] = hi
                lo_ref[begin + at : begin + at + STRIP, :] = (
                    value - hi.astype(jnp.float32)
                ).astype(jnp.bfloat16)

    def apply(tile, hi_ref, lo_ref):
        col, row = entry_of(tile)
        top = jnp.dot(left[col], hi_ref[...], preferred_element_type=jnp.float32)
        rest = jnp.dot(left[col, 0:base], lo_ref[...], preferred_element_type=jnp.float32)
        acc[row] += factor[tile + 1] * (top[:base] + top[base:] + rest)

    slots = [[ref[kind, k] for kind in ("hi", "lo", "near")] for k in range(2)]

    @pl.when(end > first)
    def _():
        for array in slots[1][:2]:
            array[...] = jnp.zeros(array.shape, array.dtype)
        spread(first, slots[0][2])

        def several(i, carry):
            for k in range(UNROLL):
                tile = first + UNROLL * i + k
                here, there = slots[k % 2], slots[(k + 1) % 2]
                build(tile, *here)
                apply(tile - 1, *there[:2])
                spread(tile + 1, there[2])
            return carry

        count = end - first
        lax.fori_loop(0, count // UNROLL, several, 0)
        done = first + count // UNROLL * UNROLL
        if UNROLL > 2:

            def pair(i, carry):
                for k in range(2):
                    tile = done + 2 * i + k
                    here, there = slots[k % 2], slots[(k + 1) % 2]
                    build(tile, *here)
                    apply(tile - 1, *there[:2])
                    spread(tile + 1, there[2])
                return carry

            lax.fori_loop(0, lax.shift_right_logical(end - done, 1), pair, 0)
        odd = jnp.bitwise_and(count, 1) == 1

        @pl.when(odd)
        def _():
            build(end - 1, *slots[0])
            apply(end - 2, *slots[1][:2])
            apply(end - 1, *slots[0][:2])

        @pl.when(jnp.logical_not(odd))
        def _():
            apply(end - 1, *slots[1][:2])

    for g in outs:
        index = groups.index(g)
        if part == "head" and g != 0:
            index = jnp.where(even, groups.index(-g), index)
        for r, span in enumerate(spans):
            ref["sum", g][:, span] = acc[2 * index + r]


def near_part(
    part, cols, first_block, width, mine, points, groups, outs, starts, ready=None, own_done=0
):
    if ready is None:
        blocks = len(cols)
    else:
        blocks = ready["left"].shape[0] // 2
    if cols:
        base, own = cols[0].shape[0] - EXTRA, cols[0].shape[1]
    else:
        base, own = starts[0].shape
    lanes = -(-2 * width // 128) * 128
    n_rows = 2 * len(groups)
    tiles = blocks * 2 * n_rows
    vmem, smem = (pl.BlockSpec(memory_space=m) for m in (pltpu.VMEM, pltpu.SMEM))
    shared = {
        "left": ((2 * blocks, 2 * base, 2 * BLOCK), jnp.bfloat16, pltpu.VMEM),
        "across": ((-(-blocks // 8), BLOCK, 128), jnp.float32, pltpu.VMEM),
        "plan": ((tiles + 8,), jnp.int32, pltpu.SMEM),
        "factor": ((tiles + 8,), jnp.float32, pltpu.SMEM),
    }
    marks = {"marks": ((2,), jnp.int32, pltpu.SMEM)}
    args, outputs, scratch = {}, {}, {}
    args["own_points"] = (mine, vmem)
    for k, value in enumerate(points):
        args["points", k] = (value, vmem)
    for s, value in enumerate(cols):
        args["col", s] = (value, vmem)
    for g, value in starts.items():
        args["start", g] = (value, vmem)
    for g in outs:
        outputs["sum", g] = ((base, own), jnp.float32, pltpu.VMEM)
    if part == "head":
        outputs |= shared | marks
    elif part == "tail":
        for name, (_, _, memory) in (shared | marks).items():
            args[name] = (ready[name], vmem if memory == pltpu.VMEM else smem)
    else:
        scratch |= shared
    for k in range(2):
        for kind in ("hi", "lo"):
            scratch[kind, k] = ((2 * BLOCK, BLOCK), jnp.bfloat16, pltpu.VMEM)
        scratch["near", k] = ((3, BLOCK, 128), jnp.float32, pltpu.VMEM)
    scratch["points"] = ((n_rows, EXTRA, BLOCK), jnp.float32, pltpu.VMEM)
    scratch["acc"] = ((n_rows, base, BLOCK), jnp.float32, pltpu.VMEM)
    if part != "tail":
        scratch["before"] = ((EXTRA, lanes), jnp.float32, pltpu.VMEM)
        scratch["tables"] = ((blocks + 2, EXTRA, lanes), jnp.float32, pltpu.SMEM)
    scratch_shapes = [memory(shape, dtype) for shape, dtype, memory in scratch.values()]
    names = [*args, *outputs, *scratch]
    if part != "tail":
        scratch_shapes.append(pltpu.SemaphoreType.DMA((blocks + 2,)))
        names.append("sem")
    spec = dict(
        blocks=blocks,
        first_block=first_block,
        width=width,
        groups=groups,
        outs=outs,
        part=part,
        own_done=own_done,
        keep=13 * blocks // 5,
        fill=FILL * blocks // 5,
        fill_last=FILL_LAST * blocks // 5,
    )
    results = pl.pallas_call(
        functools.partial(near_kernel, spec, names),
        out_shape=[jax.ShapeDtypeStruct(shape, dtype) for shape, dtype, _ in outputs.values()],
        in_specs=[place for _, place in args.values()],
        out_specs=[vmem if memory == pltpu.VMEM else smem for _, _, memory in outputs.values()],
        scratch_shapes=scratch_shapes,
        compiler_params=pltpu.CompilerParams(vmem_limit_bytes=VMEM_LIMIT),
        cost_estimate=pl.CostEstimate(
            flops=tiles * 6 * 4 * base * BLOCK * BLOCK // 2,
            bytes_accessed=4 * base * own * (blocks + 3),
            transcendentals=tiles * BLOCK * BLOCK,
        ),
    )(*(value for value, _ in args.values()))
    return dict(zip(outputs, results, strict=True))


def paired(value, first):
    count = lax.axis_size("band")
    pairs = [(i, i + 1) for i in range(first, count - 1, 2)]
    return lax.ppermute(value, "band", pairs + [(j, i) for i, j in pairs])


def swapped(value, axis, mask):
    return lax.ppermute(value, axis, [(i, i ^ mask) for i in range(lax.axis_size(axis))])


def body(drive, coords, rule_index, rule_weight, pair_cols, pair_count):
    n_dev = lax.axis_size("dev")
    patterns, own = drive.shape[1:]
    width = n_dev * (own // BLOCK)
    vmem = pl.BlockSpec(memory_space=pltpu.VMEM)
    base = 2 * patterns
    payload, mine = pl.pallas_call(
        functools.partial(pack_kernel, width),
        out_shape=[
            pltpu.VMEM((base + EXTRA, own), jnp.float32),
            pltpu.VMEM((EXTRA, own), jnp.float32),
        ],
        in_specs=[vmem] * 6,
        out_specs=[vmem] * 2,
    )(
        drive,
        coords,
        rule_index[None, :],
        rule_weight[None, :],
        pair_cols[None, :],
        pair_count[None, :],
    )
    partner = swapped(payload, "dev", 1)
    others = [swapped(payload, "dev", mask) for mask in range(2, n_dev, 2)]
    chip = [payload, partner]
    own_sum = near_part("all", chip, 0, width, mine, [], (0,), (0,), {})["sum", 0]
    outgoing, _ = lax.optimization_barrier((mine, partner))
    points = [paired(outgoing, 0), paired(outgoing, 1)]
    points, own_sum = lax.optimization_barrier((points, own_sum))
    groups = (-1, 1, 0)
    cols = chip + others[:1]
    early = near_part(
        "all", cols, 0, width, mine, points, groups, groups, {0: own_sum}, own_done=2
    )
    sums = {g: early["sum", g] for g in groups}
    others, sums = lax.optimization_barrier((others, sums))
    later = [swapped(others[0], "dev", 1)]
    for value in others[1:]:
        later += [value, swapped(value, "dev", 1)]
    head = near_part("head", later, len(cols), width, mine, points, groups, groups, sums)
    arrived = paired(head["sum", 1], 1) + paired(head["sum", -1], 0)
    tail = near_part("tail", [], 2, width, mine, [], groups, (0,), {0: head["sum", 0]}, head)
    total = (tail["sum", 0] + arrived) * mine[WEIGHT_ROW]
    return total.reshape(drive.shape)


def solution(mesh):
    spread = ("band", "dev")
    in_specs = (
        P(None, None, spread),
        P(None, spread),
        P(spread),
        P(),
        P(spread),
        P(spread),
    )
    out_specs = P(None, None, spread)
    return jax.shard_map(body, mesh=mesh, in_specs=in_specs, out_specs=out_specs, check_vma=False)
```

```python
import functools
import math

import jax
import jax.numpy as jnp
from jax import lax
from jax.experimental import pallas as pl
from jax.experimental.pallas import tpu as pltpu
from jax.sharding import PartitionSpec as P

BLOCK = 256
STRIP = 16
UNROLL = 2
COLS = 1 << 13
FILL = 16
FILL_LAST = 17
VMEM_LIMIT = 48 * 1024 * 1024

wave_number = 25.0
smoothing = 0.05
per_unit = wave_number / (2.0 * math.pi)
core_sq = (smoothing * per_unit) ** 2
amplitude = per_unit / (4.0 * math.pi)
TOP = tuple(term / 1.01171596 for term in (3.14155014, -3.02333093))
BOTTOM = tuple(term / 1.01171596 for term in (1.0, -4.25291808))

COUNT_ROW = 3
WEIGHT_ROW = 4
EXTRA = 8


def horner(z, terms):
    value = z * terms[-1] + terms[-2]
    for term in terms[-3::-1]:
        value = value * z + term
    return value


def wave(near, far):
    square = None
    for a, b in zip(near, far):
        gap = a - b
        gap = gap * gap
        square = gap + core_sq if square is None else square + gap
    inverse = lax.rsqrt(square)
    turns = square * inverse
    part = turns - jnp.round(turns)
    z = part * part
    top = horner(z, TOP) * part
    bottom = (z + BOTTOM[1]) * z + BOTTOM[0]
    top_sq, bottom_sq = top * top, bottom * bottom
    scaled = inverse * pl.reciprocal(top_sq + bottom_sq, approx=True)
    return (bottom_sq - top_sq) * scaled, (top * bottom) * scaled


def pack_kernel(width, drive, coords, rules, rule_weight, pair_cols, pair_count, out, extra):
    patterns = drive.shape[1]
    slots = pair_cols.shape[1]
    first_row = (lax.axis_index("band") * lax.axis_size("dev") + lax.axis_index("dev")) * 2
    weight = jnp.zeros(rules.shape, jnp.float32)
    for rule in range(rule_weight.shape[1]):
        weight = jnp.where(rules[...] == rule, rule_weight[0:1, rule : rule + 1], weight)
    scale = weight * amplitude
    out[0:patterns, :] = drive[0] * scale
    out[patterns : 2 * patterns, :] = drive[1] * scale
    slot = lax.broadcasted_iota(jnp.int32, (8, slots), 1)
    odd = lax.rem(slot, 2)
    place = pair_cols[...] - first_row - odd + odd * width
    place = jnp.where(slot < pair_count[...], place, -1).T[:, 0:1]
    lanes = lax.broadcasted_iota(jnp.int32, (slots, 2 * width), 1)
    counts = jnp.sum(jnp.where(lanes == place, 1.0, 0.0), axis=0, keepdims=True)
    base = 2 * patterns
    for ref, first in ((out, base), (extra, 0)):
        ref[first : first + EXTRA, :] = jnp.zeros((EXTRA, out.shape[1]), jnp.float32)
        ref[first : first + 3, :] = coords[...] * per_unit
        ref[first + COUNT_ROW : first + COUNT_ROW + 1, 0 : 2 * width] = counts
        ref[first + WEIGHT_ROW : first + WEIGHT_ROW + 1, :] = weight


def near_kernel(spec, names, *refs):
    ref = dict(zip(names, refs, strict=True))
    blocks, first_block, width, groups, outs, part = (
        spec[k] for k in ("blocks", "first_block", "width", "groups", "outs", "part")
    )
    left, across, acc, points = ref["left"], ref["across"], ref["acc"], ref["points"]
    plan = ref["plan"]
    bounds = plan.shape[0] - 2
    own_points = ref["own_points"]
    even = lax.rem(lax.axis_index("band"), 2) == 0
    base = acc.shape[1]
    half = base // 2
    spans = [slice(r * BLOCK, (r + 1) * BLOCK) for r in range(2)]

    if part != "tail":
        tables, counts, sem = ref["tables"], ref["counts"], ref["sem"]
        lanes = tables.shape[1]
        for s in range(blocks):
            row = base + COUNT_ROW
            counts[s : s + 1, :] = ref["col", s][row : row + 1, 0:lanes]
        counts[blocks : blocks + 1, :] = own_points[COUNT_ROW : COUNT_ROW + 1, 0:lanes]
        if 1 in groups:
            first, second = (
                ref["points", k][COUNT_ROW : COUNT_ROW + 1, 0:lanes] for k in range(2)
            )
            counts[blocks + 1 : blocks + 2, :] = jnp.where(even, second, first)
        copy = pltpu.make_async_copy(counts, tables, sem)
        copy.start()
        for s in range(blocks):
            for h, span in enumerate(spans):
                x = ref["col", s][0:base, span]
                turned = jnp.concatenate([-2.0 * x[half:], 2.0 * x[:half]], 0)
                wide = jnp.concatenate([x, turned], 1)
                hi = wide.astype(jnp.bfloat16)
                left[2 * s + h, 0:base, :] = hi
                left[2 * s + h, base : 2 * base, :] = (wide - hi.astype(jnp.float32)).astype(
                    jnp.bfloat16
                )
        lines = [ref["col", s][base : base + EXTRA, span] for s in range(blocks) for span in spans]
        for k in range(across.shape[0]):
            some = lines[16 * k : 16 * (k + 1)]
            spare = 128 - EXTRA * len(some)
            if spare:
                some.append(jnp.zeros((spare, BLOCK), jnp.float32))
            across[k] = jnp.concatenate(some, 0).T
    for k, g in enumerate(groups):
        for r, span in enumerate(spans):
            if g in outs:
                if ("start", g) in ref:
                    acc[2 * k + r] = ref["start", g][:, span]
                else:
                    acc[2 * k + r] = jnp.zeros(acc.shape[1:], jnp.float32)
            if g == 0:
                points[2 * k + r] = own_points[:, span]
            elif part != "tail":
                near, far = (0, 1) if g == 1 else (1, 0)
                points[2 * k + r] = jnp.where(
                    even, ref["points", near][:, span], ref["points", far][:, span]
                )
    if part != "tail":
        copy.wait()

    if part == "tail":
        first, end = plan[bounds], plan[bounds + 1]
    else:
        me = lax.axis_index("dev")
        own_line, before_line = blocks, blocks + 1

        def add(total, s, h, row, value):
            times = value.astype(jnp.int32)
            plan[total + 1] = times * COLS + (2 * s + h) * 8 + row
            return total + jnp.minimum(times, 1)

        def column_tiles(total, s, edge):
            if s + first_block == 0:
                for h in range(2):
                    for r in range(2):
                        if edge and r == h:
                            continue
                        gap = r - h
                        if edge:
                            line = before_line if gap > 0 else own_line
                            lane, row = 2 * width - 1, 2 * groups.index(-1 if gap > 0 else 1) + r
                        else:
                            line, row = own_line, 2 * groups.index(0) + r
                            lane = h * width + gap if gap >= 0 else r * width - gap
                        total = add(total, s, h, row, tables[line, lane])
                return total
            ahead = jnp.bitwise_xor(me, s + first_block) - me
            after = ahead > 0
            apart = 2 * jnp.abs(ahead)
            if edge:
                line = jnp.where(after, s, before_line)
                rows = jnp.where(after, 2 * groups.index(1), 2 * groups.index(-1))
                gap, first_is_col = width - apart, after
            else:
                line = jnp.where(after, own_line, s)
                rows = 2 * groups.index(0)
                gap, first_is_col = apart, jnp.logical_not(after)
            for h in range(2):
                for r in range(2):
                    if h == r:
                        lane = h * width + gap
                    else:
                        lane = gap + jnp.where(first_is_col, h * width + r - h, r * width + h - r)
                    total = add(total, s, h, rows + r, tables[line, lane])
            return total

        live = jnp.int32(0)
        if 1 in groups:
            for s in range(blocks):
                live = column_tiles(live, s, True)
        edge_tiles = live
        if 0 in groups:
            for s in range(spec["own_done"], blocks):
                live = column_tiles(live, s, False)
        plan[0] = 0
        plan[live + 1] = 0
        first, end = 0, live
        if part == "head":
            band, bands = lax.axis_index("band"), lax.axis_size("band")
            last = (band == 0) | (band == bands - 1)
            fill = jnp.where(last, spec["fill_last"], spec["fill"])
            end = jnp.maximum(jnp.minimum(live, fill), live - spec["keep"])
            end = jnp.maximum(edge_tiles, end)
            plan[bounds] = end
            plan[bounds + 1] = live

    def entry_of(tile):
        entry = plan[tile + 1]
        place = jnp.bitwise_and(entry, COLS - 1)
        return lax.shift_right_logical(place, 3), jnp.bitwise_and(place, 7)

    def spread(tile, near_ref):
        col, _ = entry_of(tile)
        group = lax.shift_right_logical(col, 4)
        lane = EXTRA * jnp.bitwise_and(col, 15)
        for k in range(3):
            pick = jnp.full((8, 128), lane + k, jnp.int32)
            for at in range(0, BLOCK, 8):
                near_ref[k, at : at + 8, :] = jnp.take_along_axis(
                    across[group, at : at + 8, :], pick, axis=1, mode="promise_in_bounds"
                )

    def build(tile, hi_ref, lo_ref, near_ref):
        _, row = entry_of(tile)
        far = [points[row, k : k + 1, :] for k in range(3)]
        times = BLOCK // near_ref.shape[2]
        for at in range(0, BLOCK, STRIP):
            near = [jnp.concatenate([near_ref[k, at : at + STRIP, :]] * times, 1) for k in range(3)]
            for value, begin in zip(wave(near, far), (0, BLOCK)):
                hi = value.astype(jnp.bfloat16)
                hi_ref[begin + at : begin + at + STRIP, :] = hi
                lo_ref[begin + at : begin + at + STRIP, :] = (
                    value - hi.astype(jnp.float32)
                ).astype(jnp.bfloat16)

    def apply(tile, hi_ref, lo_ref):
        col, row = entry_of(tile)
        top = jnp.dot(left[col], hi_ref[...], preferred_element_type=jnp.float32)
        rest = jnp.dot(left[col, 0:base], lo_ref[...], preferred_element_type=jnp.float32)
        times = lax.shift_right_logical(plan[tile + 1], 13).astype(jnp.float32)
        acc[row] += times * (top[:base] + top[base:] + rest)

    slots = [[ref[kind, k] for kind in ("hi", "lo", "near")] for k in range(2)]

    @pl.when(end > first)
    def _():
        for array in slots[1][:2]:
            array[...] = jnp.zeros(array.shape, array.dtype)
        spread(first, slots[0][2])

        def several(i, carry):
            for k in range(UNROLL):
                tile = first + UNROLL * i + k
                here, there = slots[k % 2], slots[(k + 1) % 2]
                build(tile, *here)
                apply(tile - 1, *there[:2])
                spread(tile + 1, there[2])
            return carry

        count = end - first
        lax.fori_loop(0, count // UNROLL, several, 0)
        done = first + count // UNROLL * UNROLL
        if UNROLL > 2:

            def pair(i, carry):
                for k in range(2):
                    tile = done + 2 * i + k
                    here, there = slots[k % 2], slots[(k + 1) % 2]
                    build(tile, *here)
                    apply(tile - 1, *there[:2])
                    spread(tile + 1, there[2])
                return carry

            lax.fori_loop(0, lax.shift_right_logical(end - done, 1), pair, 0)
        odd = jnp.bitwise_and(count, 1) == 1

        @pl.when(odd)
        def _():
            build(end - 1, *slots[0])
            apply(end - 2, *slots[1][:2])
            apply(end - 1, *slots[0][:2])

        @pl.when(jnp.logical_not(odd))
        def _():
            apply(end - 1, *slots[1][:2])

    for g in outs:
        index = groups.index(g)
        if part == "head" and g != 0:
            index = jnp.where(even, groups.index(-g), index)
        for r, span in enumerate(spans):
            ref["sum", g][:, span] = acc[2 * index + r]


def near_part(
    part, cols, first_block, width, mine, points, groups, outs, starts, ready=None, own_done=0
):
    if ready is None:
        blocks = len(cols)
    else:
        blocks = ready["left"].shape[0] // 2
    if cols:
        base, own = cols[0].shape[0] - EXTRA, cols[0].shape[1]
    else:
        base, own = starts[0].shape
    lanes = -(-2 * width // 128) * 128
    n_rows = 2 * len(groups)
    tiles = blocks * 2 * n_rows
    vmem, smem = (pl.BlockSpec(memory_space=m) for m in (pltpu.VMEM, pltpu.SMEM))
    shared = {
        "left": ((2 * blocks, 2 * base, 2 * BLOCK), jnp.bfloat16, pltpu.VMEM),
        "across": ((-(-blocks // 8), BLOCK, 128), jnp.float32, pltpu.VMEM),
        "plan": ((tiles + 8,), jnp.int32, pltpu.SMEM),
    }
    args, outputs, scratch = {}, {}, {}
    args["own_points"] = (mine, vmem)
    for k, value in enumerate(points):
        args["points", k] = (value, vmem)
    for s, value in enumerate(cols):
        args["col", s] = (value, vmem)
    for g, value in starts.items():
        args["start", g] = (value, vmem)
    for g in outs:
        outputs["sum", g] = ((base, own), jnp.float32, pltpu.VMEM)
    if part == "head":
        outputs |= shared
    elif part == "tail":
        for name, (_, _, memory) in shared.items():
            args[name] = (ready[name], vmem if memory == pltpu.VMEM else smem)
    else:
        scratch |= shared
    for k in range(2):
        for kind in ("hi", "lo"):
            scratch[kind, k] = ((2 * BLOCK, BLOCK), jnp.bfloat16, pltpu.VMEM)
        scratch["near", k] = ((3, BLOCK, 128), jnp.float32, pltpu.VMEM)
    scratch["points"] = ((n_rows, EXTRA, BLOCK), jnp.float32, pltpu.VMEM)
    scratch["acc"] = ((n_rows, base, BLOCK), jnp.float32, pltpu.VMEM)
    if part != "tail":
        lines = -(-(blocks + 2) // 8) * 8
        scratch["counts"] = ((lines, lanes), jnp.float32, pltpu.VMEM)
        scratch["tables"] = ((lines, lanes), jnp.float32, pltpu.SMEM)
    scratch_shapes = [memory(shape, dtype) for shape, dtype, memory in scratch.values()]
    names = [*args, *outputs, *scratch]
    if part != "tail":
        scratch_shapes.append(pltpu.SemaphoreType.DMA)
        names.append("sem")
    spec = dict(
        blocks=blocks,
        first_block=first_block,
        width=width,
        groups=groups,
        outs=outs,
        part=part,
        own_done=own_done,
        keep=13 * blocks // 5,
        fill=FILL * blocks // 5,
        fill_last=FILL_LAST * blocks // 5,
    )
    results = pl.pallas_call(
        functools.partial(near_kernel, spec, names),
        out_shape=[jax.ShapeDtypeStruct(shape, dtype) for shape, dtype, _ in outputs.values()],
        in_specs=[place for _, place in args.values()],
        out_specs=[vmem if memory == pltpu.VMEM else smem for _, _, memory in outputs.values()],
        scratch_shapes=scratch_shapes,
        compiler_params=pltpu.CompilerParams(vmem_limit_bytes=VMEM_LIMIT),
        cost_estimate=pl.CostEstimate(
            flops=tiles * 6 * 4 * base * BLOCK * BLOCK // 2,
            bytes_accessed=4 * base * own * (blocks + 3),
            transcendentals=tiles * BLOCK * BLOCK,
        ),
    )(*(value for value, _ in args.values()))
    return dict(zip(outputs, results, strict=True))


def paired(value, first):
    count = lax.axis_size("band")
    pairs = [(i, i + 1) for i in range(first, count - 1, 2)]
    return lax.ppermute(value, "band", pairs + [(j, i) for i, j in pairs])


def swapped(value, axis, mask):
    return lax.ppermute(value, axis, [(i, i ^ mask) for i in range(lax.axis_size(axis))])


def body(drive, coords, rule_index, rule_weight, pair_cols, pair_count):
    n_dev = lax.axis_size("dev")
    patterns, own = drive.shape[1:]
    width = n_dev * (own // BLOCK)
    vmem = pl.BlockSpec(memory_space=pltpu.VMEM)
    base = 2 * patterns
    payload, mine = pl.pallas_call(
        functools.partial(pack_kernel, width),
        out_shape=[
            pltpu.VMEM((base + EXTRA, own), jnp.float32),
            pltpu.VMEM((EXTRA, own), jnp.float32),
        ],
        in_specs=[vmem] * 6,
        out_specs=[vmem] * 2,
    )(
        drive,
        coords,
        rule_index[None, :],
        rule_weight[None, :],
        pair_cols[None, :],
        pair_count[None, :],
    )
    partner = swapped(payload, "dev", 1)
    others = [swapped(payload, "dev", mask) for mask in range(2, n_dev, 2)]
    chip = [payload, partner]
    own_sum = near_part("all", chip, 0, width, mine, [], (0,), (0,), {})["sum", 0]
    outgoing, _ = lax.optimization_barrier((mine, partner))
    points = [paired(outgoing, 0), paired(outgoing, 1)]
    points, own_sum = lax.optimization_barrier((points, own_sum))
    groups = (-1, 1, 0)
    cols = chip + others[:1]
    early = near_part(
        "all", cols, 0, width, mine, points, groups, groups, {0: own_sum}, own_done=2
    )
    sums = {g: early["sum", g] for g in groups}
    others, sums = lax.optimization_barrier((others, sums))
    later = [swapped(others[0], "dev", 1)]
    for value in others[1:]:
        later += [value, swapped(value, "dev", 1)]
    head = near_part("head", later, len(cols), width, mine, points, groups, groups, sums)
    arrived = paired(head["sum", 1], 1) + paired(head["sum", -1], 0)
    tail = near_part("tail", [], 2, width, mine, [], groups, (0,), {0: head["sum", 0]}, head)
    total = (tail["sum", 0] + arrived) * mine[WEIGHT_ROW]
    return total.reshape(drive.shape)


def solution(mesh):
    spread = ("band", "dev")
    in_specs = (
        P(None, None, spread),
        P(None, spread),
        P(spread),
        P(),
        P(spread),
        P(spread),
    )
    out_specs = P(None, None, spread)
    return jax.shard_map(body, mesh=mesh, in_specs=in_specs, out_specs=out_specs, check_vma=False)
```

```python
import functools
import math

import jax
import jax.numpy as jnp
from jax import lax
from jax.experimental import pallas as pl
from jax.experimental.pallas import tpu as pltpu
from jax.sharding import PartitionSpec as P

BLOCK = 256
STRIP = 16
UNROLL = 2
COLS = 1 << 13
FILL = 16
FILL_LAST = 17
VMEM_LIMIT = 48 * 1024 * 1024

wave_number = 25.0
smoothing = 0.05
per_unit = wave_number / (2.0 * math.pi)
core_sq = (smoothing * per_unit) ** 2
amplitude = per_unit / (4.0 * math.pi)
TOP = tuple(term / 1.01171596 for term in (3.14155014, -3.02333093))
BOTTOM = tuple(term / 1.01171596 for term in (1.0, -4.25291808))

COUNT_ROW = 3
WEIGHT_ROW = 4
EXTRA = 8


def horner(z, terms):
    value = z * terms[-1] + terms[-2]
    for term in terms[-3::-1]:
        value = value * z + term
    return value


def wave(near, far):
    square = None
    for a, b in zip(near, far):
        gap = a - b
        gap = gap * gap
        square = gap + core_sq if square is None else square + gap
    inverse = lax.rsqrt(square)
    turns = square * inverse
    part = turns - jnp.round(turns)
    z = part * part
    top = horner(z, TOP) * part
    bottom = (z + BOTTOM[1]) * z + BOTTOM[0]
    top_sq, bottom_sq = top * top, bottom * bottom
    scaled = inverse * pl.reciprocal(top_sq + bottom_sq, approx=True)
    return (bottom_sq - top_sq) * scaled, (top * bottom) * scaled


def pack_kernel(width, drive, coords, rules, rule_weight, pair_cols, pair_count, out, extra):
    patterns = drive.shape[1]
    slots = pair_cols.shape[1]
    first_row = (lax.axis_index("band") * lax.axis_size("dev") + lax.axis_index("dev")) * 2
    weight = jnp.zeros(rules.shape, jnp.float32)
    for rule in range(rule_weight.shape[1]):
        weight = jnp.where(rules[...] == rule, rule_weight[0:1, rule : rule + 1], weight)
    scale = weight * amplitude
    out[0:patterns, :] = drive[0] * scale
    out[patterns : 2 * patterns, :] = drive[1] * scale
    slot = lax.broadcasted_iota(jnp.int32, (8, slots), 1)
    odd = lax.rem(slot, 2)
    place = pair_cols[...] - first_row - odd + odd * width
    place = jnp.where(slot < pair_count[...], place, -1).T[:, 0:1]
    lanes = lax.broadcasted_iota(jnp.int32, (slots, 2 * width), 1)
    counts = jnp.sum(jnp.where(lanes == place, 1.0, 0.0), axis=0, keepdims=True)
    base = 2 * patterns
    for ref, first in ((out, base), (extra, 0)):
        ref[first : first + EXTRA, :] = jnp.zeros((EXTRA, out.shape[1]), jnp.float32)
        ref[first : first + 3, :] = coords[...] * per_unit
        ref[first + COUNT_ROW : first + COUNT_ROW + 1, 0 : 2 * width] = counts
        ref[first + WEIGHT_ROW : first + WEIGHT_ROW + 1, :] = weight


def near_kernel(spec, names, *refs):
    ref = dict(zip(names, refs, strict=True))
    blocks, first_block, width, groups, outs, part = (
        spec[k] for k in ("blocks", "first_block", "width", "groups", "outs", "part")
    )
    left, across, acc, points = ref["left"], ref["across"], ref["acc"], ref["points"]
    plan = ref["plan"]
    bounds = plan.shape[0] - 2
    own_points = ref["own_points"]
    even = lax.rem(lax.axis_index("band"), 2) == 0
    base = acc.shape[1]
    half = base // 2
    spans = [slice(r * BLOCK, (r + 1) * BLOCK) for r in range(2)]

    if part != "tail":
        tables, counts, sem = ref["tables"], ref["counts"], ref["sem"]
        lanes = tables.shape[1]
        for s in range(blocks):
            row = base + COUNT_ROW
            counts[s : s + 1, :] = ref["col", s][row : row + 1, 0:lanes]
        counts[blocks : blocks + 1, :] = own_points[COUNT_ROW : COUNT_ROW + 1, 0:lanes]
        if 1 in groups:
            first, second = (
                ref["points", k][COUNT_ROW : COUNT_ROW + 1, 0:lanes] for k in range(2)
            )
            counts[blocks + 1 : blocks + 2, :] = jnp.where(even, second, first)
        copy = pltpu.make_async_copy(counts, tables, sem)
        copy.start()
        def operands(s):
            for h, span in enumerate(spans):
                x = ref["col", s][0:base, span]
                turned = jnp.concatenate([-2.0 * x[half:], 2.0 * x[:half]], 0)
                wide = jnp.concatenate([x, turned], 1)
                hi = wide.astype(jnp.bfloat16)
                left[2 * s + h, 0:base, :] = hi
                left[2 * s + h, base : 2 * base, :] = (wide - hi.astype(jnp.float32)).astype(
                    jnp.bfloat16
                )

        for s in range(blocks // 3):
            operands(s)
        lines = [ref["col", s][base : base + EXTRA, span] for s in range(blocks) for span in spans]
        for k in range(across.shape[0]):
            some = lines[16 * k : 16 * (k + 1)]
            spare = 128 - EXTRA * len(some)
            if spare:
                some.append(jnp.zeros((spare, BLOCK), jnp.float32))
            across[k] = jnp.concatenate(some, 0).T
    for k, g in enumerate(groups):
        for r, span in enumerate(spans):
            if g in outs:
                if ("start", g) in ref:
                    acc[2 * k + r] = ref["start", g][:, span]
                else:
                    acc[2 * k + r] = jnp.zeros(acc.shape[1:], jnp.float32)
            if g == 0:
                points[2 * k + r] = own_points[:, span]
            elif part != "tail":
                near, far = (0, 1) if g == 1 else (1, 0)
                points[2 * k + r] = jnp.where(
                    even, ref["points", near][:, span], ref["points", far][:, span]
                )
    if part != "tail":
        copy.wait()
        for s in range(blocks // 3, blocks):
            operands(s)

    if part == "tail":
        first, end = plan[bounds], plan[bounds + 1]
    else:
        me = lax.axis_index("dev")
        own_line, before_line = blocks, blocks + 1

        def add(total, s, h, row, value):
            times = value.astype(jnp.int32)
            plan[total + 1] = times * COLS + (2 * s + h) * 8 + row
            return total + jnp.minimum(times, 1)

        def column_tiles(total, s, edge):
            if s + first_block == 0:
                for h in range(2):
                    for r in range(2):
                        if edge and r == h:
                            continue
                        gap = r - h
                        if edge:
                            line = before_line if gap > 0 else own_line
                            lane, row = 2 * width - 1, 2 * groups.index(-1 if gap > 0 else 1) + r
                        else:
                            line, row = own_line, 2 * groups.index(0) + r
                            lane = h * width + gap if gap >= 0 else r * width - gap
                        total = add(total, s, h, row, tables[line, lane])
                return total
            ahead = jnp.bitwise_xor(me, s + first_block) - me
            after = ahead > 0
            apart = 2 * jnp.abs(ahead)
            if edge:
                line = jnp.where(after, s, before_line)
                rows = jnp.where(after, 2 * groups.index(1), 2 * groups.index(-1))
                gap, first_is_col = width - apart, after
            else:
                line = jnp.where(after, own_line, s)
                rows = 2 * groups.index(0)
                gap, first_is_col = apart, jnp.logical_not(after)
            for h in range(2):
                for r in range(2):
                    if h == r:
                        lane = h * width + gap
                    else:
                        lane = gap + jnp.where(first_is_col, h * width + r - h, r * width + h - r)
                    total = add(total, s, h, rows + r, tables[line, lane])
            return total

        live = jnp.int32(0)
        if 1 in groups:
            for s in range(blocks):
                live = column_tiles(live, s, True)
        edge_tiles = live
        if 0 in groups:
            for s in range(spec["own_done"], blocks):
                live = column_tiles(live, s, False)
        plan[0] = 0
        plan[live + 1] = 0
        first, end = 0, live
        if part == "head":
            band, bands = lax.axis_index("band"), lax.axis_size("band")
            last = (band == 0) | (band == bands - 1)
            fill = jnp.where(last, spec["fill_last"], spec["fill"])
            end = jnp.maximum(jnp.minimum(live, fill), live - spec["keep"])
            end = jnp.maximum(edge_tiles, end)
            plan[bounds] = end
            plan[bounds + 1] = live

    def entry_of(tile):
        entry = plan[tile + 1]
        place = jnp.bitwise_and(entry, COLS - 1)
        return lax.shift_right_logical(place, 3), jnp.bitwise_and(place, 7)

    def spread(tile, near_ref):
        col, _ = entry_of(tile)
        group = lax.shift_right_logical(col, 4)
        lane = EXTRA * jnp.bitwise_and(col, 15)
        for k in range(3):
            pick = jnp.full((8, 128), lane + k, jnp.int32)
            for at in range(0, BLOCK, 8):
                near_ref[k, at : at + 8, :] = jnp.take_along_axis(
                    across[group, at : at + 8, :], pick, axis=1, mode="promise_in_bounds"
                )

    def build(tile, hi_ref, lo_ref, near_ref):
        _, row = entry_of(tile)
        far = [points[row, k : k + 1, :] for k in range(3)]
        times = BLOCK // near_ref.shape[2]
        for at in range(0, BLOCK, STRIP):
            near = [jnp.concatenate([near_ref[k, at : at + STRIP, :]] * times, 1) for k in range(3)]
            for value, begin in zip(wave(near, far), (0, BLOCK)):
                hi = value.astype(jnp.bfloat16)
                hi_ref[begin + at : begin + at + STRIP, :] = hi
                lo_ref[begin + at : begin + at + STRIP, :] = (
                    value - hi.astype(jnp.float32)
                ).astype(jnp.bfloat16)

    def apply(tile, hi_ref, lo_ref):
        col, row = entry_of(tile)
        top = jnp.dot(left[col], hi_ref[...], preferred_element_type=jnp.float32)
        rest = jnp.dot(left[col, 0:base], lo_ref[...], preferred_element_type=jnp.float32)
        times = lax.shift_right_logical(plan[tile + 1], 13).astype(jnp.float32)
        acc[row] += times * (top[:base] + top[base:] + rest)

    slots = [[ref[kind, k] for kind in ("hi", "lo", "near")] for k in range(2)]

    @pl.when(end > first)
    def _():
        for array in slots[1][:2]:
            array[...] = jnp.zeros(array.shape, array.dtype)
        spread(first, slots[0][2])

        def several(i, carry):
            for k in range(UNROLL):
                tile = first + UNROLL * i + k
                here, there = slots[k % 2], slots[(k + 1) % 2]
                build(tile, *here)
                apply(tile - 1, *there[:2])
                spread(tile + 1, there[2])
            return carry

        count = end - first
        lax.fori_loop(0, count // UNROLL, several, 0)
        done = first + count // UNROLL * UNROLL
        if UNROLL > 2:

            def pair(i, carry):
                for k in range(2):
                    tile = done + 2 * i + k
                    here, there = slots[k % 2], slots[(k + 1) % 2]
                    build(tile, *here)
                    apply(tile - 1, *there[:2])
                    spread(tile + 1, there[2])
                return carry

            lax.fori_loop(0, lax.shift_right_logical(end - done, 1), pair, 0)
        odd = jnp.bitwise_and(count, 1) == 1

        @pl.when(odd)
        def _():
            build(end - 1, *slots[0])
            apply(end - 2, *slots[1][:2])
            apply(end - 1, *slots[0][:2])

        @pl.when(jnp.logical_not(odd))
        def _():
            apply(end - 1, *slots[1][:2])

    for g in outs:
        index = groups.index(g)
        if part == "head" and g != 0:
            index = jnp.where(even, groups.index(-g), index)
        for r, span in enumerate(spans):
            ref["sum", g][:, span] = acc[2 * index + r]


def near_part(
    part, cols, first_block, width, mine, points, groups, outs, starts, ready=None, own_done=0
):
    if ready is None:
        blocks = len(cols)
    else:
        blocks = ready["left"].shape[0] // 2
    if cols:
        base, own = cols[0].shape[0] - EXTRA, cols[0].shape[1]
    else:
        base, own = starts[0].shape
    lanes = -(-2 * width // 128) * 128
    n_rows = 2 * len(groups)
    tiles = blocks * 2 * n_rows
    vmem, smem = (pl.BlockSpec(memory_space=m) for m in (pltpu.VMEM, pltpu.SMEM))
    shared = {
        "left": ((2 * blocks, 2 * base, 2 * BLOCK), jnp.bfloat16, pltpu.VMEM),
        "across": ((-(-blocks // 8), BLOCK, 128), jnp.float32, pltpu.VMEM),
        "plan": ((tiles + 8,), jnp.int32, pltpu.SMEM),
    }
    args, outputs, scratch = {}, {}, {}
    args["own_points"] = (mine, vmem)
    for k, value in enumerate(points):
        args["points", k] = (value, vmem)
    for s, value in enumerate(cols):
        args["col", s] = (value, vmem)
    for g, value in starts.items():
        args["start", g] = (value, vmem)
    for g in outs:
        outputs["sum", g] = ((base, own), jnp.float32, pltpu.VMEM)
    if part == "head":
        outputs |= shared
    elif part == "tail":
        for name, (_, _, memory) in shared.items():
            args[name] = (ready[name], vmem if memory == pltpu.VMEM else smem)
    else:
        scratch |= shared
    for k in range(2):
        for kind in ("hi", "lo"):
            scratch[kind, k] = ((2 * BLOCK, BLOCK), jnp.bfloat16, pltpu.VMEM)
        scratch["near", k] = ((3, BLOCK, 128), jnp.float32, pltpu.VMEM)
    scratch["points"] = ((n_rows, EXTRA, BLOCK), jnp.float32, pltpu.VMEM)
    scratch["acc"] = ((n_rows, base, BLOCK), jnp.float32, pltpu.VMEM)
    if part != "tail":
        lines = -(-(blocks + 2) // 8) * 8
        scratch["counts"] = ((lines, lanes), jnp.float32, pltpu.VMEM)
        scratch["tables"] = ((lines, lanes), jnp.float32, pltpu.SMEM)
    scratch_shapes = [memory(shape, dtype) for shape, dtype, memory in scratch.values()]
    names = [*args, *outputs, *scratch]
    if part != "tail":
        scratch_shapes.append(pltpu.SemaphoreType.DMA)
        names.append("sem")
    spec = dict(
        blocks=blocks,
        first_block=first_block,
        width=width,
        groups=groups,
        outs=outs,
        part=part,
        own_done=own_done,
        keep=13 * blocks // 5,
        fill=FILL * blocks // 5,
        fill_last=FILL_LAST * blocks // 5,
    )
    results = pl.pallas_call(
        functools.partial(near_kernel, spec, names),
        out_shape=[jax.ShapeDtypeStruct(shape, dtype) for shape, dtype, _ in outputs.values()],
        in_specs=[place for _, place in args.values()],
        out_specs=[vmem if memory == pltpu.VMEM else smem for _, _, memory in outputs.values()],
        scratch_shapes=scratch_shapes,
        compiler_params=pltpu.CompilerParams(vmem_limit_bytes=VMEM_LIMIT),
        cost_estimate=pl.CostEstimate(
            flops=tiles * 6 * 4 * base * BLOCK * BLOCK // 2,
            bytes_accessed=4 * base * own * (blocks + 3),
            transcendentals=tiles * BLOCK * BLOCK,
        ),
    )(*(value for value, _ in args.values()))
    return dict(zip(outputs, results, strict=True))


def paired(value, first):
    count = lax.axis_size("band")
    pairs = [(i, i + 1) for i in range(first, count - 1, 2)]
    return lax.ppermute(value, "band", pairs + [(j, i) for i, j in pairs])


def swapped(value, axis, mask):
    return lax.ppermute(value, axis, [(i, i ^ mask) for i in range(lax.axis_size(axis))])


def body(drive, coords, rule_index, rule_weight, pair_cols, pair_count):
    n_dev = lax.axis_size("dev")
    patterns, own = drive.shape[1:]
    width = n_dev * (own // BLOCK)
    vmem = pl.BlockSpec(memory_space=pltpu.VMEM)
    base = 2 * patterns
    payload, mine = pl.pallas_call(
        functools.partial(pack_kernel, width),
        out_shape=[
            pltpu.VMEM((base + EXTRA, own), jnp.float32),
            pltpu.VMEM((EXTRA, own), jnp.float32),
        ],
        in_specs=[vmem] * 6,
        out_specs=[vmem] * 2,
    )(
        drive,
        coords,
        rule_index[None, :],
        rule_weight[None, :],
        pair_cols[None, :],
        pair_count[None, :],
    )
    partner = swapped(payload, "dev", 1)
    others = [swapped(payload, "dev", mask) for mask in range(2, n_dev, 2)]
    chip = [payload, partner]
    own_sum = near_part("all", chip, 0, width, mine, [], (0,), (0,), {})["sum", 0]
    outgoing, _ = lax.optimization_barrier((mine, partner))
    points = [paired(outgoing, 0), paired(outgoing, 1)]
    points, own_sum = lax.optimization_barrier((points, own_sum))
    groups = (-1, 1, 0)
    cols = chip + others[:1]
    early = near_part(
        "all", cols, 0, width, mine, points, groups, groups, {0: own_sum}, own_done=2
    )
    sums = {g: early["sum", g] for g in groups}
    others, sums = lax.optimization_barrier((others, sums))
    later = [swapped(others[0], "dev", 1)]
    for value in others[1:]:
        later += [value, swapped(value, "dev", 1)]
    head = near_part("head", later, len(cols), width, mine, points, groups, groups, sums)
    arrived = paired(head["sum", 1], 1) + paired(head["sum", -1], 0)
    tail = near_part("tail", [], 2, width, mine, [], groups, (0,), {0: head["sum", 0]}, head)
    total = (tail["sum", 0] + arrived) * mine[WEIGHT_ROW]
    return total.reshape(drive.shape)


def solution(mesh):
    spread = ("band", "dev")
    in_specs = (
        P(None, None, spread),
        P(None, spread),
        P(spread),
        P(),
        P(spread),
        P(spread),
    )
    out_specs = P(None, None, spread)
    return jax.shard_map(body, mesh=mesh, in_specs=in_specs, out_specs=out_specs, check_vma=False)
```

```python
import functools
import math

import jax
import jax.numpy as jnp
from jax import lax
from jax.experimental import pallas as pl
from jax.experimental.pallas import tpu as pltpu
from jax.sharding import PartitionSpec as P

BLOCK = 256
STRIP = 16
UNROLL = 2
COLS = 1 << 13
FILL = 16
FILL_LAST = 17
VMEM_LIMIT = 48 * 1024 * 1024

wave_number = 25.0
smoothing = 0.05
per_unit = wave_number / (2.0 * math.pi)
core_sq = (smoothing * per_unit) ** 2
amplitude = per_unit / (4.0 * math.pi)
TOP = tuple(term / 1.01171596 for term in (3.14155014, -3.02333093))
BOTTOM = tuple(term / 1.01171596 for term in (1.0, -4.25291808))

COUNT_ROW = 3
WEIGHT_ROW = 4
EXTRA = 8


def horner(z, terms):
    value = z * terms[-1] + terms[-2]
    for term in terms[-3::-1]:
        value = value * z + term
    return value


def wave(near, far):
    square = None
    for a, b in zip(near, far):
        gap = a - b
        gap = gap * gap
        square = gap + core_sq if square is None else square + gap
    inverse = lax.rsqrt(square)
    turns = square * inverse
    part = turns - jnp.round(turns)
    z = part * part
    top = horner(z, TOP) * part
    bottom = (z + BOTTOM[1]) * z + BOTTOM[0]
    top_sq, bottom_sq = top * top, bottom * bottom
    scaled = inverse * pl.reciprocal(top_sq + bottom_sq, approx=True)
    return (bottom_sq - top_sq) * scaled, (top * bottom) * scaled


def pack_kernel(width, drive, coords, rules, rule_weight, pair_cols, pair_count, out, extra):
    patterns = drive.shape[1]
    slots = pair_cols.shape[1]
    first_row = (lax.axis_index("band") * lax.axis_size("dev") + lax.axis_index("dev")) * 2
    weight = jnp.zeros(rules.shape, jnp.float32)
    for rule in range(rule_weight.shape[1]):
        weight = jnp.where(rules[...] == rule, rule_weight[0:1, rule : rule + 1], weight)
    scale = weight * amplitude
    out[0:patterns, :] = drive[0] * scale
    out[patterns : 2 * patterns, :] = drive[1] * scale
    slot = lax.broadcasted_iota(jnp.int32, (8, slots), 1)
    odd = lax.rem(slot, 2)
    place = pair_cols[...] - first_row - odd + odd * width
    place = jnp.where(slot < pair_count[...], place, -1).T[:, 0:1]
    lanes = lax.broadcasted_iota(jnp.int32, (slots, 2 * width), 1)
    counts = jnp.sum(jnp.where(lanes == place, 1.0, 0.0), axis=0, keepdims=True)
    base = 2 * patterns
    for ref, first in ((out, base), (extra, 0)):
        ref[first : first + EXTRA, :] = jnp.zeros((EXTRA, out.shape[1]), jnp.float32)
        ref[first : first + 3, :] = coords[...] * per_unit
        ref[first + COUNT_ROW : first + COUNT_ROW + 1, 0 : 2 * width] = counts
        ref[first + WEIGHT_ROW : first + WEIGHT_ROW + 1, :] = weight


def near_kernel(spec, names, *refs):
    ref = dict(zip(names, refs, strict=True))
    blocks, first_block, width, groups, outs, part = (
        spec[k] for k in ("blocks", "first_block", "width", "groups", "outs", "part")
    )
    left, across, acc, points = ref["left"], ref["across"], ref["acc"], ref["points"]
    plan = ref["plan"]
    bounds = plan.shape[0] - 2
    own_points = ref["own_points"]
    even = lax.rem(lax.axis_index("band"), 2) == 0
    base = acc.shape[1]
    half = base // 2
    spans = [slice(r * BLOCK, (r + 1) * BLOCK) for r in range(2)]

    if part != "tail":
        tables, counts, sem = ref["tables"], ref["counts"], ref["sem"]
        lanes = tables.shape[1]
        for s in range(blocks):
            row = base + COUNT_ROW
            counts[s : s + 1, :] = ref["col", s][row : row + 1, 0:lanes]
        counts[blocks : blocks + 1, :] = own_points[COUNT_ROW : COUNT_ROW + 1, 0:lanes]
        if 1 in groups:
            first, second = (
                ref["points", k][COUNT_ROW : COUNT_ROW + 1, 0:lanes] for k in range(2)
            )
            counts[blocks + 1 : blocks + 2, :] = jnp.where(even, second, first)
        copy = pltpu.make_async_copy(counts, tables, sem)
        copy.start()
        def operands(s):
            for h, span in enumerate(spans):
                x = ref["col", s][0:base, span]
                hi = x.astype(jnp.bfloat16)
                lo = (x - hi.astype(jnp.float32)).astype(jnp.bfloat16)
                for part_of, begin in ((hi, 0), (lo, base)):
                    double = part_of + part_of
                    turned = jnp.concatenate([-double[half:], double[:half]], 0)
                    left[2 * s + h, begin : begin + base, :] = jnp.concatenate(
                        [part_of, turned], 1
                    )

        for s in range(blocks // 3):
            operands(s)
        lines = [ref["col", s][base : base + EXTRA, span] for s in range(blocks) for span in spans]
        for k in range(across.shape[0]):
            some = lines[16 * k : 16 * (k + 1)]
            spare = 128 - EXTRA * len(some)
            if spare:
                some.append(jnp.zeros((spare, BLOCK), jnp.float32))
            across[k] = jnp.concatenate(some, 0).T
    for k, g in enumerate(groups):
        for r, span in enumerate(spans):
            if g in outs:
                if ("start", g) in ref:
                    acc[2 * k + r] = ref["start", g][:, span]
                else:
                    acc[2 * k + r] = jnp.zeros(acc.shape[1:], jnp.float32)
            if g == 0:
                points[2 * k + r] = own_points[:, span]
            elif part != "tail":
                near, far = (0, 1) if g == 1 else (1, 0)
                points[2 * k + r] = jnp.where(
                    even, ref["points", near][:, span], ref["points", far][:, span]
                )
    if part != "tail":
        copy.wait()
        for s in range(blocks // 3, blocks):
            operands(s)

    if part == "tail":
        first, end = plan[bounds], plan[bounds + 1]
    else:
        me = lax.axis_index("dev")
        own_line, before_line = blocks, blocks + 1

        def add(total, s, h, row, value):
            times = value.astype(jnp.int32)
            plan[total + 1] = times * COLS + (2 * s + h) * 8 + row
            return total + jnp.minimum(times, 1)

        def column_tiles(total, s, edge):
            if s + first_block == 0:
                for h in range(2):
                    for r in range(2):
                        if edge and r == h:
                            continue
                        gap = r - h
                        if edge:
                            line = before_line if gap > 0 else own_line
                            lane, row = 2 * width - 1, 2 * groups.index(-1 if gap > 0 else 1) + r
                        else:
                            line, row = own_line, 2 * groups.index(0) + r
                            lane = h * width + gap if gap >= 0 else r * width - gap
                        total = add(total, s, h, row, tables[line, lane])
                return total
            ahead = jnp.bitwise_xor(me, s + first_block) - me
            after = ahead > 0
            apart = 2 * jnp.abs(ahead)
            if edge:
                line = jnp.where(after, s, before_line)
                rows = jnp.where(after, 2 * groups.index(1), 2 * groups.index(-1))
                gap, first_is_col = width - apart, after
            else:
                line = jnp.where(after, own_line, s)
                rows = 2 * groups.index(0)
                gap, first_is_col = apart, jnp.logical_not(after)
            for h in range(2):
                for r in range(2):
                    if h == r:
                        lane = h * width + gap
                    else:
                        lane = gap + jnp.where(first_is_col, h * width + r - h, r * width + h - r)
                    total = add(total, s, h, rows + r, tables[line, lane])
            return total

        live = jnp.int32(0)
        if 1 in groups:
            for s in range(blocks):
                live = column_tiles(live, s, True)
        edge_tiles = live
        if 0 in groups:
            for s in range(spec["own_done"], blocks):
                live = column_tiles(live, s, False)
        plan[0] = 0
        plan[live + 1] = 0
        first, end = 0, live
        if part == "head":
            band, bands = lax.axis_index("band"), lax.axis_size("band")
            last = (band == 0) | (band == bands - 1)
            fill = jnp.where(last, spec["fill_last"], spec["fill"])
            end = jnp.maximum(jnp.minimum(live, fill), live - spec["keep"])
            end = jnp.maximum(edge_tiles, end)
            plan[bounds] = end
            plan[bounds + 1] = live

    def entry_of(tile):
        entry = plan[tile + 1]
        place = jnp.bitwise_and(entry, COLS - 1)
        return lax.shift_right_logical(place, 3), jnp.bitwise_and(place, 7)

    def spread(tile, near_ref):
        col, _ = entry_of(tile)
        group = lax.shift_right_logical(col, 4)
        lane = EXTRA * jnp.bitwise_and(col, 15)
        for k in range(3):
            pick = jnp.full((8, 128), lane + k, jnp.int32)
            for at in range(0, BLOCK, 8):
                near_ref[k, at : at + 8, :] = jnp.take_along_axis(
                    across[group, at : at + 8, :], pick, axis=1, mode="promise_in_bounds"
                )

    def build(tile, hi_ref, lo_ref, near_ref):
        _, row = entry_of(tile)
        far = [points[row, k : k + 1, :] for k in range(3)]
        times = BLOCK // near_ref.shape[2]
        for at in range(0, BLOCK, STRIP):
            near = [jnp.concatenate([near_ref[k, at : at + STRIP, :]] * times, 1) for k in range(3)]
            for value, begin in zip(wave(near, far), (0, BLOCK)):
                hi = value.astype(jnp.bfloat16)
                hi_ref[begin + at : begin + at + STRIP, :] = hi
                lo_ref[begin + at : begin + at + STRIP, :] = (
                    value - hi.astype(jnp.float32)
                ).astype(jnp.bfloat16)

    def apply(tile, hi_ref, lo_ref):
        col, row = entry_of(tile)
        top = jnp.dot(left[col], hi_ref[...], preferred_element_type=jnp.float32)
        rest = jnp.dot(left[col, 0:base], lo_ref[...], preferred_element_type=jnp.float32)
        times = lax.shift_right_logical(plan[tile + 1], 13).astype(jnp.float32)
        acc[row] += times * (top[:base] + top[base:] + rest)

    slots = [[ref[kind, k] for kind in ("hi", "lo", "near")] for k in range(2)]

    @pl.when(end > first)
    def _():
        for array in slots[1][:2]:
            array[...] = jnp.zeros(array.shape, array.dtype)
        spread(first, slots[0][2])

        def several(i, carry):
            for k in range(UNROLL):
                tile = first + UNROLL * i + k
                here, there = slots[k % 2], slots[(k + 1) % 2]
                build(tile, *here)
                apply(tile - 1, *there[:2])
                spread(tile + 1, there[2])
            return carry

        count = end - first
        lax.fori_loop(0, count // UNROLL, several, 0)
        done = first + count // UNROLL * UNROLL
        if UNROLL > 2:

            def pair(i, carry):
                for k in range(2):
                    tile = done + 2 * i + k
                    here, there = slots[k % 2], slots[(k + 1) % 2]
                    build(tile, *here)
                    apply(tile - 1, *there[:2])
                    spread(tile + 1, there[2])
                return carry

            lax.fori_loop(0, lax.shift_right_logical(end - done, 1), pair, 0)
        odd = jnp.bitwise_and(count, 1) == 1

        @pl.when(odd)
        def _():
            build(end - 1, *slots[0])
            apply(end - 2, *slots[1][:2])
            apply(end - 1, *slots[0][:2])

        @pl.when(jnp.logical_not(odd))
        def _():
            apply(end - 1, *slots[1][:2])

    for g in outs:
        index = groups.index(g)
        if part == "head" and g != 0:
            index = jnp.where(even, groups.index(-g), index)
        for r, span in enumerate(spans):
            ref["sum", g][:, span] = acc[2 * index + r]


def near_part(
    part, cols, first_block, width, mine, points, groups, outs, starts, ready=None, own_done=0
):
    if ready is None:
        blocks = len(cols)
    else:
        blocks = ready["left"].shape[0] // 2
    if cols:
        base, own = cols[0].shape[0] - EXTRA, cols[0].shape[1]
    else:
        base, own = starts[0].shape
    lanes = -(-2 * width // 128) * 128
    n_rows = 2 * len(groups)
    tiles = blocks * 2 * n_rows
    vmem, smem = (pl.BlockSpec(memory_space=m) for m in (pltpu.VMEM, pltpu.SMEM))
    shared = {
        "left": ((2 * blocks, 2 * base, 2 * BLOCK), jnp.bfloat16, pltpu.VMEM),
        "across": ((-(-blocks // 8), BLOCK, 128), jnp.float32, pltpu.VMEM),
        "plan": ((tiles + 8,), jnp.int32, pltpu.SMEM),
    }
    args, outputs, scratch = {}, {}, {}
    args["own_points"] = (mine, vmem)
    for k, value in enumerate(points):
        args["points", k] = (value, vmem)
    for s, value in enumerate(cols):
        args["col", s] = (value, vmem)
    for g, value in starts.items():
        args["start", g] = (value, vmem)
    for g in outs:
        outputs["sum", g] = ((base, own), jnp.float32, pltpu.VMEM)
    if part == "head":
        outputs |= shared
    elif part == "tail":
        for name, (_, _, memory) in shared.items():
            args[name] = (ready[name], vmem if memory == pltpu.VMEM else smem)
    else:
        scratch |= shared
    for k in range(2):
        for kind in ("hi", "lo"):
            scratch[kind, k] = ((2 * BLOCK, BLOCK), jnp.bfloat16, pltpu.VMEM)
        scratch["near", k] = ((3, BLOCK, 128), jnp.float32, pltpu.VMEM)
    scratch["points"] = ((n_rows, EXTRA, BLOCK), jnp.float32, pltpu.VMEM)
    scratch["acc"] = ((n_rows, base, BLOCK), jnp.float32, pltpu.VMEM)
    if part != "tail":
        lines = -(-(blocks + 2) // 8) * 8
        scratch["counts"] = ((lines, lanes), jnp.float32, pltpu.VMEM)
        scratch["tables"] = ((lines, lanes), jnp.float32, pltpu.SMEM)
    scratch_shapes = [memory(shape, dtype) for shape, dtype, memory in scratch.values()]
    names = [*args, *outputs, *scratch]
    if part != "tail":
        scratch_shapes.append(pltpu.SemaphoreType.DMA)
        names.append("sem")
    spec = dict(
        blocks=blocks,
        first_block=first_block,
        width=width,
        groups=groups,
        outs=outs,
        part=part,
        own_done=own_done,
        keep=13 * blocks // 5,
        fill=FILL * blocks // 5,
        fill_last=FILL_LAST * blocks // 5,
    )
    results = pl.pallas_call(
        functools.partial(near_kernel, spec, names),
        out_shape=[jax.ShapeDtypeStruct(shape, dtype) for shape, dtype, _ in outputs.values()],
        in_specs=[place for _, place in args.values()],
        out_specs=[vmem if memory == pltpu.VMEM else smem for _, _, memory in outputs.values()],
        scratch_shapes=scratch_shapes,
        compiler_params=pltpu.CompilerParams(vmem_limit_bytes=VMEM_LIMIT),
        cost_estimate=pl.CostEstimate(
            flops=tiles * 6 * 4 * base * BLOCK * BLOCK // 2,
            bytes_accessed=4 * base * own * (blocks + 3),
            transcendentals=tiles * BLOCK * BLOCK,
        ),
    )(*(value for value, _ in args.values()))
    return dict(zip(outputs, results, strict=True))


def paired(value, first):
    count = lax.axis_size("band")
    pairs = [(i, i + 1) for i in range(first, count - 1, 2)]
    return lax.ppermute(value, "band", pairs + [(j, i) for i, j in pairs])


def swapped(value, axis, mask):
    return lax.ppermute(value, axis, [(i, i ^ mask) for i in range(lax.axis_size(axis))])


def body(drive, coords, rule_index, rule_weight, pair_cols, pair_count):
    n_dev = lax.axis_size("dev")
    patterns, own = drive.shape[1:]
    width = n_dev * (own // BLOCK)
    vmem = pl.BlockSpec(memory_space=pltpu.VMEM)
    base = 2 * patterns
    payload, mine = pl.pallas_call(
        functools.partial(pack_kernel, width),
        out_shape=[
            pltpu.VMEM((base + EXTRA, own), jnp.float32),
            pltpu.VMEM((EXTRA, own), jnp.float32),
        ],
        in_specs=[vmem] * 6,
        out_specs=[vmem] * 2,
    )(
        drive,
        coords,
        rule_index[None, :],
        rule_weight[None, :],
        pair_cols[None, :],
        pair_count[None, :],
    )
    partner = swapped(payload, "dev", 1)
    others = [swapped(payload, "dev", mask) for mask in range(2, n_dev, 2)]
    chip = [payload, partner]
    own_sum = near_part("all", chip, 0, width, mine, [], (0,), (0,), {})["sum", 0]
    outgoing, _ = lax.optimization_barrier((mine, partner))
    points = [paired(outgoing, 0), paired(outgoing, 1)]
    points, own_sum = lax.optimization_barrier((points, own_sum))
    groups = (-1, 1, 0)
    cols = chip + others[:1]
    early = near_part(
        "all", cols, 0, width, mine, points, groups, groups, {0: own_sum}, own_done=2
    )
    sums = {g: early["sum", g] for g in groups}
    others, sums = lax.optimization_barrier((others, sums))
    later = [swapped(others[0], "dev", 1)]
    for value in others[1:]:
        later += [value, swapped(value, "dev", 1)]
    head = near_part("head", later, len(cols), width, mine, points, groups, groups, sums)
    arrived = paired(head["sum", 1], 1) + paired(head["sum", -1], 0)
    tail = near_part("tail", [], 2, width, mine, [], groups, (0,), {0: head["sum", 0]}, head)
    total = (tail["sum", 0] + arrived) * mine[WEIGHT_ROW]
    return total.reshape(drive.shape)


def solution(mesh):
    spread = ("band", "dev")
    in_specs = (
        P(None, None, spread),
        P(None, spread),
        P(spread),
        P(),
        P(spread),
        P(spread),
    )
    out_specs = P(None, None, spread)
    return jax.shard_map(body, mesh=mesh, in_specs=in_specs, out_specs=out_specs, check_vma=False)
```
